128 devices in a mesh: series: 16 (over x, y), patch: 8 (over z, core).
Axes of the slice: x: 4, y: 4, z: 4, core: 2. Of those that a mesh axis runs over, the one named last changes fastest.
Arguments:
- series_data: bfloat16 [256, 512, 768], P(('series', 'patch')), may hold values from -6 to 6
- group_id: int32 [256], replicated, may hold values from 0 to 63, as said below
- gains: bfloat16 [3, 768], replicated, may hold values from 0.099609375 to 1.8984375
- w_time: bfloat16 [768, 2304], replicated, may hold values from -0.21875 to 0.21875
- w_time_out: bfloat16 [768, 768], replicated, may hold values from -0.21875 to 0.21875
- w_group: bfloat16 [768, 2304], replicated, may hold values from -0.21875 to 0.21875
- w_group_out: bfloat16 [768, 768], replicated, may hold values from -0.21875 to 0.21875
- w_up: bfloat16 [768, 3072], replicated, may hold values from -0.21875 to 0.21875
- w_down: bfloat16 [3072, 768], replicated, may hold values from -0.109375 to 0.109375
Outputs:
- layer_out: bfloat16 [256, 512, 768], P(('series', 'patch'))
The draws below stay inside these ranges and needn't reach their ends.
Inputs may be any that keep to these rules, and one draw needn't show every extreme that they name: `group_id`: group ids never fall along the series and rise by at most one from a series to the next; a new group begins at every multiple of 16, and each aligned block of 16 series holds the same number of groups, a quarter of 16 but at least two; group sizes are ragged.
All inputs are finite; a program needn't handle non-finite values.
Results may differ from the reference program's by a relative error of at most 0.019.
Values may be sent and summed in bfloat16 or wider, within the bound.
No kernel may reach another device: no remote copies, remote signals or barrier semaphores. Data moves between devices by JAX's collectives and lax.ppermute only.
A program may use at most 128 MiB of HBM per device.

```python
import math
import jax
import jax.numpy as jnp
from jax import lax

D = 768
HEADS = 12
FF = 3072
PATCHES = 512
SERIES = 256
BLOCK = 16


def block_flags(block_key, groups_each):
    shuffled = jax.random.permutation(block_key, BLOCK - 1) + 1
    flags = jnp.zeros((BLOCK,), jnp.int32).at[0].set(1)
    return flags.at[shuffled[:groups_each - 1]].set(1)


def draw_group_id(key, part):
    key = jax.random.fold_in(key, 7)
    block_count = SERIES // BLOCK
    groups_each = max(BLOCK // 4, 2)
    block_keys = jax.random.split(key, block_count)
    flags = jax.vmap(lambda single: block_flags(single, groups_each))(block_keys).reshape(SERIES)
    return (jnp.cumsum(flags) - 1).astype(jnp.int32)


def block_levels(own_key, extent, cuts, smallest, high):
    level = 1.0
    for position, blocks in cuts:
        steps = jax.random.uniform(jax.random.fold_in(jax.random.fold_in(own_key, 6), position), (blocks,), jnp.float32, smallest / len(cuts), high / len(cuts))
        level = level * jnp.repeat(jnp.exp(steps), extent[position] // blocks).reshape((-1,) + (1,) * (len(extent) - 1 - position))
    return level


def normal_values(rng, dims, scale, most, cuts=(), kind=jnp.bfloat16):
    values = jax.random.normal(rng, dims, jnp.float32) * scale
    if len(cuts) > 0:
        values = block_levels(rng, dims, cuts, -0.22, 0.18) * values
    return jnp.clip(values, min=-most, max=most).astype(kind)


def setup_inputs(seed: int = 0) -> dict:
    seeds = jax.random.split(jax.random.key(seed), 10)
    return {
        "series_data": normal_values(seeds[0], (SERIES, PATCHES, D), 1.0, 6.0, ((0, 128),)),
        "group_id": draw_group_id(jax.random.fold_in(seeds[9], 71), 0),
        "gains": jnp.clip(1.0 + 0.18 * jax.random.normal(seeds[2], (3, D), jnp.float32), 0.099609375, 1.8984375).astype(jnp.bfloat16),
        "w_time": normal_values(seeds[3], (D, 3 * D), D ** -0.5, 0.21875),
        "w_time_out": normal_values(seeds[4], (D, D), D ** -0.5, 0.21875),
        "w_group": normal_values(seeds[5], (D, 3 * D), D ** -0.5, 0.21875),
        "w_group_out": normal_values(seeds[6], (D, D), D ** -0.5, 0.21875),
        "w_up": normal_values(seeds[7], (D, FF), D ** -0.5, 0.21875),
        "w_down": normal_values(seeds[8], (FF, D), FF ** -0.5, 0.109375),
    }


EPSILON = 1e-06

def normed(inputs, gain_row):
    values = inputs.astype(jnp.float32)
    mean_square = lax.optimization_barrier(jnp.mean(values * values, axis=-1, keepdims=True))
    return (values * lax.rsqrt(mean_square + EPSILON) * gain_row.astype(jnp.float32)).astype(jnp.bfloat16)

def rotate(tensor, length):
    half_size = tensor.shape[-1] // 2
    frequency = 10000.0 ** (-jnp.arange(half_size, dtype=jnp.float32) / half_size)
    angles = jnp.arange(length, dtype=jnp.float32)[:, None] * frequency[None, :]
    cosine = jnp.cos(angles)[:, None, :]
    sine_part = jnp.sin(angles)[:, None, :]
    front_half = tensor[..., :half_size]
    back_half = tensor[..., half_size:]
    return jnp.concatenate([front_half * cosine - back_half * sine_part, front_half * sine_part + back_half * cosine], axis=-1)

def time_block(inputs, gain_row, w_time, w_time_out):
    batch_count, length, model_width = inputs.shape
    head_size = model_width // HEADS
    flattened = normed(inputs, gain_row).reshape(batch_count * length, model_width)
    projected = jnp.dot(flattened, w_time, preferred_element_type=jnp.float32).reshape(batch_count, length, 3, HEADS, head_size)
    queries = rotate(projected[:, :, 0], length).astype(jnp.bfloat16)
    key_heads = rotate(projected[:, :, 1], length).astype(jnp.bfloat16)
    values = projected[:, :, 2].astype(jnp.bfloat16)
    scores = jnp.einsum('bqhe,bkhe->bhqk', queries.astype(jnp.float32), key_heads.astype(jnp.float32)) / math.sqrt(head_size)
    weights = jax.nn.softmax(scores, axis=-1).astype(jnp.bfloat16)
    context = jnp.einsum('bhqk,bkhe->bqhe', weights.astype(jnp.float32), values.astype(jnp.float32)).astype(jnp.bfloat16)
    update = jnp.dot(context.reshape(batch_count * length, model_width), w_time_out, preferred_element_type=jnp.float32)
    residual = inputs.reshape(batch_count * length, model_width).astype(jnp.float32)
    return (residual + update).astype(jnp.bfloat16).reshape(batch_count, length, model_width)

def group_block(inputs, group_ids, gain_row, w_group, w_group_out):
    series_count, length, model_width = inputs.shape
    head_size = model_width // HEADS
    flattened = normed(inputs, gain_row).reshape(series_count * length, model_width)
    projected = jnp.dot(flattened, w_group, preferred_element_type=jnp.float32).reshape(series_count, length, 3, HEADS, head_size)
    queries = projected[:, :, 0].astype(jnp.bfloat16)
    key_heads = projected[:, :, 1].astype(jnp.bfloat16)
    values = projected[:, :, 2].astype(jnp.bfloat16)
    scores = jnp.einsum('sphe,tphe->phst', queries.astype(jnp.float32), key_heads.astype(jnp.float32)) / math.sqrt(head_size)
    same_group = group_ids[:, None] == group_ids[None, :]
    scores = jnp.where(same_group[None, None], scores, -1e+30)
    weights = jax.nn.softmax(scores, axis=-1).astype(jnp.bfloat16)
    context = jnp.einsum('phst,tphe->sphe', weights.astype(jnp.float32), values.astype(jnp.float32)).astype(jnp.bfloat16)
    update = jnp.dot(context.reshape(series_count * length, model_width), w_group_out, preferred_element_type=jnp.float32)
    residual = inputs.reshape(series_count * length, model_width).astype(jnp.float32)
    return (residual + update).astype(jnp.bfloat16).reshape(series_count, length, model_width)

def feed_forward(inputs, gain_row, w_up, w_down):
    hidden = jax.nn.gelu(jnp.dot(normed(inputs, gain_row), w_up, preferred_element_type=jnp.float32), approximate=False).astype(jnp.bfloat16)
    return (inputs.astype(jnp.float32) + jnp.dot(hidden, w_down, preferred_element_type=jnp.float32)).astype(jnp.bfloat16)

def reference(series_data, group_id, gains, w_time, w_time_out, w_group, w_group_out, w_up, w_down):

    def one_series(single):
        return time_block(single[None], gains[0], w_time, w_time_out)[0]
    after_time = lax.map(one_series, series_data)

    def one_patch(column):
        return group_block(column[:, None, :], group_id, gains[1], w_group, w_group_out)[:, 0, :]
    after_group = jnp.swapaxes(lax.map(one_patch, jnp.swapaxes(after_time, 0, 1)), 0, 1)

    def one_block(row_block):
        return feed_forward(row_block, gains[2], w_up, w_down)
    return lax.map(one_block, after_group)
```

```python
import functools
import math

import jax
import jax.numpy as jnp
import numpy as np
from jax import lax
from jax.experimental import pallas as pl
from jax.experimental.pallas import tpu as pltpu
from jax.sharding import PartitionSpec as P

HEADS = 12
HEAD = 64
SLAB = 128
QUAD = 256
EPSILON = 1e-06
CHUNKS = 2
BLOCK = 16
BF16, F32 = jnp.bfloat16, jnp.float32
VMEM_LIMIT = 40 * 1024 * 1024

TAIL = (
    -1.0000376231361372,
    -1.1507878484871916,
    -0.4599924445285111,
    -0.05182737928832041,
    0.00708455624965549,
    -0.00047330922195818663,
)


def dot(a, b):
    return jnp.dot(a, b, preferred_element_type=F32)


def dot_t(a, b):
    return lax.dot_general(a, b, (((1,), (1,)), ((), ())), preferred_element_type=F32)


def normed(values, gain_row):
    values = values.astype(F32)
    mean_square = jnp.mean(values * values, axis=-1, keepdims=True)
    return (values * lax.rsqrt(mean_square + EPSILON) * gain_row).astype(BF16)


def gelu(x):
    size = jnp.abs(x)
    tail = jnp.full_like(size, TAIL[-1])
    for coefficient in TAIL[-2::-1]:
        tail = tail * size + coefficient
    return jnp.maximum(x, 0.0) - size * jnp.exp2(tail)


def rotary_tables(length):
    half = HEAD // 2
    frequency = 10000.0 ** (-np.arange(half) / half)
    angles = np.arange(length)[:, None] * frequency[None, :]
    cosine, sine = np.cos(angles), np.sin(angles)
    cosine = np.concatenate([cosine] * 4, axis=1).astype(np.float32)
    sine = np.concatenate([-sine, sine, -sine, sine], axis=1).astype(np.float32)
    return cosine, sine


def rotated(tensor, cosine, sine, scale=None):
    lane = lax.broadcasted_iota(jnp.int32, (tensor.shape[0], SLAB), 1)
    front = lax.rem(lane, HEAD) < HEAD // 2
    parts = []
    for start in range(0, tensor.shape[1], SLAB):
        slab = tensor[:, start : start + SLAB]
        other = jnp.where(front, pltpu.roll(slab, SLAB - 32, 1), pltpu.roll(slab, 32, 1))
        turned = slab * cosine + other * sine
        if scale is not None:
            turned = turned * scale
        parts.append(turned.astype(BF16))
    return jnp.concatenate(parts, axis=1)


QUERY_SCALE = math.log2(math.e) / math.sqrt(HEAD)


def slab_attention(queries, keys, values, bias=None):
    first = lax.broadcasted_iota(jnp.int32, queries.shape, 1) < HEAD
    extended = jnp.concatenate([values, jnp.ones_like(values)], axis=1)
    zero = jnp.zeros_like(queries)
    results = []
    for own in (jnp.where(first, queries, zero), jnp.where(first, zero, queries)):
        scores = dot_t(own, keys)
        if bias is not None:
            scores = scores + bias
        top = jnp.max(scores, axis=-1, keepdims=True)
        weights = jnp.exp2(scores - top).astype(BF16)
        results.append(dot(weights, extended))
    numerator = jnp.where(first, results[0][:, :SLAB], results[1][:, :SLAB])
    denominator = jnp.where(first, results[0][:, SLAB:], results[1][:, SLAB:])
    return (numerator / denominator).astype(BF16)


def time_kernel(chunk, *refs):
    if chunk == 0:
        (x_ref, gain_ref, cos_ref, sin_ref, wq_ref, wk_ref, wv_ref, wo_ref,
         keys_ref, values_ref, mixed_ref, norm, total) = refs
    else:
        (x_ref, gain_ref, cos_ref, sin_ref, wq_ref, wo_ref, keys_ref, values_ref,
         mixed_ref, norm, total) = refs
    step = pl.program_id(0)
    series, length, width = x_ref.shape
    part = length // CHUNKS
    low = chunk * part
    gain = gain_ref[...].astype(F32)

    @pl.when(step == 0)
    def _():
        for s in range(series):
            if chunk == 0:
                norm[s] = normed(x_ref[s], gain)
            else:
                norm[s] = normed(x_ref[s, low : low + part], gain)
            total[s] = x_ref[s, low : low + part].astype(F32)

    if chunk == 0:
        for s in range(series):
            keys_ref[s] = rotated(dot(norm[s], wk_ref[...]), cos_ref[...], sin_ref[...])
            values_ref[s] = dot(norm[s], wv_ref[...]).astype(BF16)
    for s in range(series):
        queries = rotated(
            dot(norm[s, :part], wq_ref[...]),
            cos_ref[low : low + part],
            sin_ref[low : low + part],
            QUERY_SCALE,
        )
        context = []
        for start in range(0, QUAD, SLAB):
            own = slice(start, start + SLAB)
            context.append(slab_attention(queries[:, own], keys_ref[s, :, own], values_ref[s, :, own]))
        total[s] += dot(jnp.concatenate(context, axis=1), wo_ref[...])

    @pl.when(step == pl.num_programs(0) - 1)
    def _():
        for s in range(series):
            mixed_ref[:, s] = total[s].astype(BF16).reshape(mixed_ref.shape[0], -1, width)


def time_chunk(chunk, devices, x, gain, tables, w_time, w_time_out, keys=None, values=None):
    series, length, width = x.shape
    part = length // CHUNKS
    quads = width // QUAD
    whole = lambda shape: pl.BlockSpec(shape, lambda j: (0,) * len(shape))
    columns = lambda first: pl.BlockSpec((width, QUAD), lambda j: (0, first + j))
    heads = pl.BlockSpec((series, length, QUAD), lambda j: (0, 0, j))
    in_specs = [whole(x.shape), whole(gain.shape), whole(tables[0].shape), whole(tables[1].shape)]
    operands = [x, gain, *tables]
    out_w = pl.BlockSpec((QUAD, width), lambda j: (j, 0))
    mixed_shape = (devices, series, part // devices, width)
    mixed_out = jax.ShapeDtypeStruct(mixed_shape, BF16)
    like = jax.ShapeDtypeStruct(x.shape, BF16)
    rows = series * part
    flops = 2 * rows * width * width * 2 + 4 * rows * length * width
    if chunk == 0:
        in_specs += [columns(0), columns(quads), columns(2 * quads), out_w]
        operands += [w_time, w_time, w_time, w_time_out]
        out_shape = [like, like, mixed_out]
        out_specs = [heads, heads, whole(mixed_shape)]
        flops += 2 * series * length * width * width * 2
    else:
        in_specs += [columns(0), out_w, heads, heads]
        operands += [w_time, w_time_out, keys, values]
        out_shape = mixed_out
        out_specs = whole(mixed_shape)
    return pl.pallas_call(
        functools.partial(time_kernel, chunk),
        grid=(quads,),
        in_specs=in_specs,
        out_specs=out_specs,
        out_shape=out_shape,
        scratch_shapes=[
            pltpu.VMEM((series, length if chunk == 0 else part, width), BF16),
            pltpu.VMEM((series, part, width), F32),
        ],
        compiler_params=pltpu.CompilerParams(vmem_limit_bytes=VMEM_LIMIT),
        cost_estimate=pl.CostEstimate(
            flops=flops, bytes_accessed=8 << 20, transcendentals=rows * length * HEADS
        ),
        name=f"time_attention_{chunk}",
    )(*operands)


def group_kernel(ids_ref, x_ref, gain_ref, wq_ref, wk_ref, wv_ref, wo_ref, out_ref, norm, total, bias):
    step = pl.program_id(0)
    block, patches, width = x_ref.shape
    tiles = patches // BLOCK
    rows = block * BLOCK

    @pl.when(step == 0)
    def _():
        gain = gain_ref[...].astype(F32)
        for t in range(tiles):
            own = x_ref[:, t * BLOCK : (t + 1) * BLOCK].reshape(rows, width)
            norm[t * rows : (t + 1) * rows] = normed(own, gain)
            total[t * rows : (t + 1) * rows] = own.astype(F32)
        row = lax.broadcasted_iota(jnp.int32, (rows, rows), 0)
        column = lax.broadcasted_iota(jnp.int32, (rows, rows), 1)
        row_series, column_series = row // BLOCK, column // BLOCK
        row_group, column_group = jnp.zeros_like(row), jnp.zeros_like(row)
        for s in range(block):
            row_group = jnp.where(row_series == s, ids_ref[s], row_group)
            column_group = jnp.where(column_series == s, ids_ref[s], column_group)
        same = jnp.logical_and(row_group == column_group, lax.rem(row, BLOCK) == lax.rem(column, BLOCK))
        bias[...] = jnp.where(same, 0.0, -1e30)

    queries = (dot(norm[...], wq_ref[...]) * QUERY_SCALE).astype(BF16)
    keys = dot(norm[...], wk_ref[...]).astype(BF16)
    values = dot(norm[...], wv_ref[...]).astype(BF16)
    for t in range(tiles):
        own = slice(t * rows, (t + 1) * rows)
        context = []
        for start in range(0, QUAD, SLAB):
            lanes = slice(start, start + SLAB)
            context.append(
                slab_attention(queries[own, lanes], keys[own, lanes], values[own, lanes], bias[...])
            )
        total[own] += dot(jnp.concatenate(context, axis=1), wo_ref[...])

    @pl.when(step == pl.num_programs(0) - 1)
    def _():
        for t in range(tiles):
            result = total[t * rows : (t + 1) * rows].astype(BF16)
            out_ref[:, t * BLOCK : (t + 1) * BLOCK] = result.reshape(block, BLOCK, width)


def group_chunk(chunk, x, ids, gain, w_group, w_group_out):
    block, patches, width = x.shape
    quads = width // QUAD
    rows = block * patches
    whole = lambda shape: pl.BlockSpec(shape, lambda j: (0,) * len(shape))
    columns = lambda first: pl.BlockSpec((width, QUAD), lambda j: (0, first + j))
    return pl.pallas_call(
        group_kernel,
        grid=(quads,),
        in_specs=[
            pl.BlockSpec(memory_space=pltpu.SMEM),
            whole(x.shape),
            whole(gain.shape),
            columns(0),
            columns(quads),
            columns(2 * quads),
            pl.BlockSpec((QUAD, width), lambda j: (j, 0)),
        ],
        out_specs=whole(x.shape),
        out_shape=jax.ShapeDtypeStruct(x.shape, BF16),
        scratch_shapes=[
            pltpu.VMEM((rows, width), BF16),
            pltpu.VMEM((rows, width), F32),
            pltpu.VMEM((block * BLOCK, block * BLOCK), F32),
        ],
        compiler_params=pltpu.CompilerParams(vmem_limit_bytes=VMEM_LIMIT),
        cost_estimate=pl.CostEstimate(
            flops=2 * rows * width * width * 4 + 4 * rows * 256 * width,
            bytes_accessed=8 << 20,
            transcendentals=rows * 256 * HEADS,
        ),
        name=f"group_attention_{chunk}",
    )(ids, x, gain, w_group, w_group, w_group, w_group_out)


FF_TILE = 512


def feed_kernel(*refs):
    x_ref, gain_ref, up_ref, down_ref = refs[:4]
    out_ref, norm, total = refs[-3:]
    step = pl.program_id(0)
    devices, series, patches, width = x_ref.shape
    rows = devices * patches

    @pl.when(step == 0)
    def _():
        gain = gain_ref[...].astype(F32)
        for s in range(series):
            own = x_ref[:, s].reshape(rows, width)
            norm[s * rows : (s + 1) * rows] = normed(own, gain)
            total[s * rows : (s + 1) * rows] = own.astype(F32)

    for s in range(series):
        own = slice(s * rows, (s + 1) * rows)
        hidden = gelu(dot(norm[own], up_ref[...])).astype(BF16)
        total[own] += dot(hidden, down_ref[...])

    @pl.when(step == pl.num_programs(0) - 1)
    def _():
        for s in range(series):
            out_ref[s] = total[s * rows : (s + 1) * rows].astype(BF16)


def feed_chunk(chunk, x, gain, w_up, w_down, out=None):
    devices, series, patches, width = x.shape
    hidden = w_up.shape[1]
    part = devices * patches
    rows = series * part
    whole = lambda shape: pl.BlockSpec(shape, lambda j: (0,) * len(shape))
    in_specs = [
        whole(x.shape),
        whole(gain.shape),
        pl.BlockSpec((width, FF_TILE), lambda j: (0, j)),
        pl.BlockSpec((FF_TILE, width), lambda j: (j, 0)),
    ]
    operands = [x, gain, w_up, w_down]
    if out is not None:
        in_specs.append(pl.BlockSpec(memory_space=pl.ANY))
        operands.append(out)
    return pl.pallas_call(
        feed_kernel,
        grid=(hidden // FF_TILE,),
        in_specs=in_specs,
        out_specs=pl.BlockSpec((series, part, width), lambda j: (0, chunk, 0)),
        out_shape=jax.ShapeDtypeStruct((series, CHUNKS * part, width), BF16),
        scratch_shapes=[pltpu.VMEM((rows, width), BF16), pltpu.VMEM((rows, width), F32)],
        input_output_aliases={} if out is None else {4: 0},
        compiler_params=pltpu.CompilerParams(vmem_limit_bytes=VMEM_LIMIT),
        cost_estimate=pl.CostEstimate(
            flops=4 * rows * width * hidden, bytes_accessed=12 << 20, transcendentals=rows * hidden
        ),
        name=f"feed_forward_{chunk}",
    )(*operands)


def exchanged(blocks):
    return lax.all_to_all(blocks, "patch", split_axis=0, concat_axis=0)


def per_device(
    series_data, group_id, gains, w_time, w_time_out, w_group, w_group_out, w_up, w_down
):
    devices = lax.axis_size("patch")
    series, length, width = series_data.shape
    block = devices * series
    ids = lax.dynamic_slice(group_id, (lax.axis_index("series") * block,), (block,))
    tables = rotary_tables(length)
    gain = [gains[i : i + 1] for i in range(3)]

    keys, values, mixed_a = time_chunk(0, devices, series_data, gain[0], tables, w_time, w_time_out)
    there_a = exchanged(mixed_a)
    mixed_b = time_chunk(
        1, devices, series_data, gain[0], tables, w_time, w_time_out, keys, values
    )
    there_b = exchanged(mixed_b)
    shape = there_a.shape
    joined = (block, shape[2], width)
    group_a = group_chunk(0, there_a.reshape(joined), ids, gain[1], w_group, w_group_out)
    back_a = exchanged(group_a.reshape(shape))
    group_b = group_chunk(1, there_b.reshape(joined), ids, gain[1], w_group, w_group_out)
    back_b = exchanged(group_b.reshape(shape))
    out = feed_chunk(0, back_a, gain[2], w_up, w_down)
    return feed_chunk(1, back_b, gain[2], w_up, w_down, out)


def solution(mesh):
    in_specs = (P(("series", "patch"), None, None), P(), P(), P(), P(), P(), P(), P(), P())
    out_specs = P(("series", "patch"), None, None)
    return jax.shard_map(
        per_device, mesh=mesh, in_specs=in_specs, out_specs=out_specs, check_vma=False
    )
```

```python
import functools
import math

import jax
import jax.numpy as jnp
import numpy as np
from jax import lax
from jax.experimental import pallas as pl
from jax.experimental.pallas import tpu as pltpu
from jax.sharding import PartitionSpec as P

HEADS = 12
HEAD = 64
SLAB = 128
QUAD = 256
EPSILON = 1e-06
CHUNKS = 2
BLOCK = 16
BF16, F32 = jnp.bfloat16, jnp.float32
VMEM_LIMIT = 60 * 1024 * 1024

TAIL = (
    -1.0000376231361372,
    -1.1507878484871916,
    -0.4599924445285111,
    -0.05182737928832041,
    0.00708455624965549,
    -0.00047330922195818663,
)


def dot(a, b):
    return jnp.dot(a, b, preferred_element_type=F32)


def dot_t(a, b):
    return lax.dot_general(a, b, (((1,), (1,)), ((), ())), preferred_element_type=F32)


def normed(values, gain_row):
    values = values.astype(F32)
    mean_square = jnp.mean(values * values, axis=-1, keepdims=True)
    return (values * lax.rsqrt(mean_square + EPSILON) * gain_row).astype(BF16)


def gelu(x):
    size = jnp.abs(x)
    tail = jnp.full_like(size, TAIL[-1])
    for coefficient in TAIL[-2::-1]:
        tail = tail * size + coefficient
    return jnp.maximum(x, 0.0) - size * jnp.exp2(tail)


def rotary_tables(length):
    half = HEAD // 2
    frequency = 10000.0 ** (-np.arange(half) / half)
    angles = np.arange(length)[:, None] * frequency[None, :]
    cosine, sine = np.cos(angles), np.sin(angles)
    cosine = np.concatenate([cosine] * 4, axis=1).astype(np.float32)
    sine = np.concatenate([-sine, sine, -sine, sine], axis=1).astype(np.float32)
    return cosine, sine


def rotated(tensor, cosine, sine, scale=None):
    lane = lax.broadcasted_iota(jnp.int32, (tensor.shape[0], SLAB), 1)
    front = lax.rem(lane, HEAD) < HEAD // 2
    parts = []
    for start in range(0, tensor.shape[1], SLAB):
        slab = tensor[:, start : start + SLAB]
        other = jnp.where(front, pltpu.roll(slab, SLAB - 32, 1), pltpu.roll(slab, 32, 1))
        turned = slab * cosine + other * sine
        if scale is not None:
            turned = turned * scale
        parts.append(turned.astype(BF16))
    return jnp.concatenate(parts, axis=1)


QUERY_SCALE = math.log2(math.e) / math.sqrt(HEAD)
HBM = pl.BlockSpec(memory_space=pltpu.HBM)
SMEM = pl.BlockSpec(memory_space=pltpu.SMEM)


def slab_scores(queries, keys):
    first = lax.broadcasted_iota(jnp.int32, queries.shape, 1) < HEAD
    zero = jnp.zeros_like(queries)
    both = jnp.concatenate([jnp.where(first, queries, zero), jnp.where(first, zero, queries)], axis=0)
    return dot_t(both, keys)


def slab_context(scores, values):
    rows = scores.shape[0] // 2
    top = jnp.max(scores, axis=-1, keepdims=True)
    weights = jnp.exp2(scores - top).astype(BF16)
    sums = dot(weights, jnp.concatenate([values, jnp.ones_like(values)], axis=1))
    first = lax.broadcasted_iota(jnp.int32, (rows, SLAB), 1) < HEAD
    numerator = jnp.where(first, sums[:rows, :SLAB], sums[rows:, :SLAB])
    denominator = jnp.where(first, sums[:rows, SLAB:], sums[rows:, SLAB:])
    return (numerator / denominator).astype(BF16)


def pipelined(units, scores_of, context_of):
    scores = scores_of(units[0])
    for index, unit in enumerate(units):
        later = scores_of(units[index + 1]) if index + 1 < len(units) else None
        context_of(unit, scores)
        scores = later


class Copies:
    def __init__(self, sems):
        self.sems, self.used = sems, 0

    def start(self, source, target):
        copy = pltpu.make_async_copy(source, target, self.sems.at[self.used])
        self.used += 1
        copy.start()
        return copy


def time_kernel(chunk, *refs):
    if chunk == 0:
        (x_ref, gains_hbm, cos_hbm, sin_hbm, w_hbm, wo_hbm,
         mixed_ref, keys_hbm, values_hbm, later_hbm,
         x, wq, wo, cosine, sine, context, mixed, keys, values, norm, gains, wk, wv, sems) = refs
    else:
        (x_ref, cos_hbm, sin_hbm, w_hbm, wo_hbm, keys_hbm, values_hbm, later_hbm,
         mixed_ref, x, wq, wo, cosine, sine, context, mixed, keys, values, norm, sems) = refs
    series, length, width = x_ref.shape
    part = length // CHUNKS
    low = chunk * part
    quads = width // QUAD
    copies = Copies(sems)
    puts = []
    needed = []
    if chunk == 0:
        get_gains = copies.start(gains_hbm, gains)
        get_x = [copies.start(x_ref.at[s], x.at[s]) for s in range(series)]
    else:
        get_norm = copies.start(later_hbm, norm)
    for j in range(quads):
        own = slice(j * QUAD, (j + 1) * QUAD)
        group = []
        for i, target in ((1, wk), (2, wv), (0, wq)) if chunk == 0 else ((0, wq),):
            lanes = slice(i * width + j * QUAD, i * width + (j + 1) * QUAD)
            group.append(copies.start(w_hbm.at[:, lanes], target.at[:, own]))
        if j == 0:
            group.append(copies.start(cos_hbm.at[low:], cosine))
            group.append(copies.start(sin_hbm.at[low:], sine))
        if chunk > 0:
            group.append(copies.start(keys_hbm.at[:, :, own], keys.at[:, :, own]))
            group.append(copies.start(values_hbm.at[:, :, own], values.at[:, :, own]))
        needed.append(group)
    get_wo = copies.start(wo_hbm, wo)
    if chunk == 0:
        get_gains.wait()
        gain = gains[0:1].astype(F32)
        for s in range(series):
            get_x[s].wait()
            norm[s] = normed(x[s], gain)
        puts.append(copies.start(norm.at[:, part:], later_hbm))
        now = norm[:, :part].reshape(series * part, width)
        everything = norm[...].reshape(series * length, width)
        residual = lambda s: x[s, :part]
    else:
        get_x = copies.start(x_ref.at[:, low:], x)
        get_norm.wait()
        now = norm[...].reshape(series * part, width)
        residual = lambda s: x[s]
    for j in range(quads):
        own = slice(j * QUAD, (j + 1) * QUAD)
        for copy in needed[j]:
            copy.wait()
        if chunk == 0:
            raw = dot(everything, wk[:, own])
            for s in range(series):
                keys[s, :, own] = rotated(raw[s * length : (s + 1) * length], cosine[...], sine[...])
            values[:, :, own] = dot(everything, wv[:, own]).astype(BF16).reshape(series, length, QUAD)
        raw = dot(now, wq[:, own])
        queries = [
            rotated(raw[s * part : (s + 1) * part], cosine[:part], sine[:part], QUERY_SCALE)
            for s in range(series)
        ]
        units = [(s, start) for start in range(0, QUAD, SLAB) for s in range(series)]

        def scores_of(unit):
            s, start = unit
            lanes = slice(j * QUAD + start, j * QUAD + start + SLAB)
            return slab_scores(queries[s][:, start : start + SLAB], keys[s, :, lanes])

        def context_of(unit, scores):
            s, start = unit
            lanes = slice(j * QUAD + start, j * QUAD + start + SLAB)
            context[s * part : (s + 1) * part, lanes] = slab_context(scores, values[s, :, lanes])

        pipelined(units, scores_of, context_of)
        if chunk == 0:
            puts.append(copies.start(keys.at[:, :, own], keys_hbm.at[:, :, own]))
            puts.append(copies.start(values.at[:, :, own], values_hbm.at[:, :, own]))

    get_wo.wait()
    if chunk > 0:
        get_x.wait()
    update = dot(context[...], wo[...])
    for s in range(series):
        result = residual(s).astype(F32) + update[s * part : (s + 1) * part]
        mixed[s] = result.astype(BF16).reshape(mixed.shape[1:])
        puts.append(copies.start(mixed.at[s], mixed_ref.at[:, s]))
    for put in puts:
        put.wait()


def params():
    return pltpu.CompilerParams(vmem_limit_bytes=VMEM_LIMIT)


def time_chunk(chunk, devices, x, gains, tables, w_time, w_time_out, kept=()):
    series, length, width = x.shape
    part = length // CHUNKS
    mixed_shape = (devices, series, part // devices, width)
    rows = series * part
    table_rows = length - chunk * part
    like = jax.ShapeDtypeStruct(x.shape, BF16)
    out_shape = [jax.ShapeDtypeStruct(mixed_shape, BF16)]
    operands = [x, *tables, w_time, w_time_out, *kept]
    scratch = [
        pltpu.VMEM((series, length if chunk == 0 else part, width), BF16),
        pltpu.VMEM((width, width), BF16),
        pltpu.VMEM((width, width), BF16),
        pltpu.VMEM((table_rows, SLAB), F32),
        pltpu.VMEM((table_rows, SLAB), F32),
        pltpu.VMEM((rows, width), BF16),
        pltpu.VMEM((series, devices, part // devices, width), BF16),
        pltpu.VMEM(x.shape, BF16),
        pltpu.VMEM(x.shape, BF16),
        pltpu.VMEM((series, length if chunk == 0 else part, width), BF16),
    ]
    flops = 2 * rows * width * width * 2 + 8 * rows * length * width
    if chunk == 0:
        operands.insert(1, gains)
        out_shape += [like, like, jax.ShapeDtypeStruct((series, length - part, width), BF16)]
        scratch += [
            pltpu.VMEM(gains.shape, BF16),
            pltpu.VMEM((width, width), BF16),
            pltpu.VMEM((width, width), BF16),
        ]
        flops += 2 * series * length * width * width * 2
    return pl.pallas_call(
        functools.partial(time_kernel, chunk),
        in_specs=[HBM] * len(operands),
        out_specs=[HBM] * len(out_shape),
        out_shape=out_shape,
        scratch_shapes=scratch + [pltpu.SemaphoreType.DMA((32,))],
        compiler_params=params(),
        cost_estimate=pl.CostEstimate(
            flops=flops, bytes_accessed=8 << 20, transcendentals=rows * length * HEADS
        ),
        name=f"time_attention_{chunk}",
    )(*operands)


FF_TILE = 512


def feed(norm, up, down, hidden):
    tiles = [slice(start, start + FF_TILE) for start in range(0, up.shape[1], FF_TILE)]
    raw = dot(norm[...], up[:, tiles[0]])
    for index, own in enumerate(tiles):
        later = dot(norm[...], up[:, tiles[index + 1]]) if index + 1 < len(tiles) else None
        hidden[:, own] = gelu(raw).astype(BF16)
        raw = later
    return dot(hidden[...], down[...])


def group_kernel(chunk, *refs):
    if chunk == 0:
        (ids, x_ref, gains_hbm, wg_hbm, wo_hbm, out_ref,
         x, norm, context, result, bias, gains, wg, wo, sems) = refs
    else:
        (ids, x_ref, gains_hbm, wg_hbm, wo_hbm, up_hbm, down_hbm, out_ref,
         x, norm, context, result, bias, gains, wg, wo, hidden, up, down, sems) = refs
    block, patches, width = x_ref.shape
    tiles = patches // BLOCK
    rows = block * BLOCK
    copies = Copies(sems)
    patches_of = lambda t: slice(t * BLOCK, (t + 1) * BLOCK)
    rows_of = lambda t: slice(t * rows, (t + 1) * rows)
    get_x = [copies.start(gains_hbm, gains)]
    get_x += [copies.start(x_ref.at[:, patches_of(t)], x.at[t]) for t in range(tiles)]
    get_w = []
    for j in range(width // QUAD):
        parts = [slice(i * width + j * QUAD, i * width + (j + 1) * QUAD) for i in range(3)]
        get_w.append([copies.start(wg_hbm.at[:, lanes], wg.at[:, lanes]) for lanes in parts])
    get_wo = copies.start(wo_hbm, wo)
    if chunk > 0:
        get_feed = [copies.start(up_hbm, up), copies.start(down_hbm, down)]

    row = lax.broadcasted_iota(jnp.int32, (rows, rows), 0)
    column = lax.broadcasted_iota(jnp.int32, (rows, rows), 1)
    row_series, column_series = row // BLOCK, column // BLOCK
    row_group, column_group = jnp.zeros_like(row), jnp.zeros_like(row)
    first_series = lax.axis_index("series") * block
    for s in range(block):
        group = ids[first_series + s]
        row_group = jnp.where(row_series == s, group, row_group)
        column_group = jnp.where(column_series == s, group, column_group)
    same = jnp.logical_and(row_group == column_group, lax.rem(row, BLOCK) == lax.rem(column, BLOCK))
    bias[...] = jnp.where(same, 0.0, -1e30)

    get_x[0].wait()
    gain = gains[1:2].astype(F32)
    for t in range(tiles):
        get_x[1 + t].wait()
        norm[rows_of(t)] = normed(x[t].reshape(rows, width), gain)
    for j in range(width // QUAD):
        for copy in get_w[j]:
            copy.wait()

        def project(i):
            return dot(norm[...], wg[:, i * width + j * QUAD : i * width + (j + 1) * QUAD])

        queries = (project(0) * QUERY_SCALE).astype(BF16)
        keys = project(1).astype(BF16)
        values = project(2).astype(BF16)

        def scores_of(unit):
            t, start = unit
            lanes = slice(start, start + SLAB)
            scores = slab_scores(queries[rows_of(t), lanes], keys[rows_of(t), lanes])
            return scores + jnp.concatenate([bias[...], bias[...]], axis=0)

        def context_of(unit, scores):
            t, start = unit
            made = slab_context(scores, values[rows_of(t), start : start + SLAB])
            context[rows_of(t), j * QUAD + start : j * QUAD + start + SLAB] = made

        units = [(t, start) for start in range(0, QUAD, SLAB) for t in range(tiles)]
        pipelined(units, scores_of, context_of)

    get_wo.wait()
    update = dot(context[...], wo[...])
    if chunk > 0:
        gain = gains[2:3].astype(F32)
        for t in range(tiles):
            total = x[t].reshape(rows, width).astype(F32) + update[rows_of(t)]
            x[t] = total.astype(BF16).reshape(block, BLOCK, width)
            norm[rows_of(t)] = normed(x[t].reshape(rows, width), gain)
        for copy in get_feed:
            copy.wait()
        update = feed(norm, up, down, hidden)
    puts = []
    for t in range(tiles):
        total = x[t].reshape(rows, width).astype(F32) + update[rows_of(t)]
        result[t] = total.astype(BF16).reshape(block, BLOCK, width)
        puts.append(copies.start(result.at[t], out_ref.at[:, patches_of(t)]))
    for copy in puts:
        copy.wait()


def group_chunk(chunk, x, ids, gains, w_group, w_group_out, *feed_weights):
    block, patches, width = x.shape
    rows = block * patches
    tiles = (patches // BLOCK, block, BLOCK, width)
    extra = [pltpu.VMEM(array.shape, BF16) for array in feed_weights]
    if extra:
        extra.insert(0, pltpu.VMEM((rows, feed_weights[0].shape[1]), BF16))
    return pl.pallas_call(
        functools.partial(group_kernel, chunk),
        in_specs=[SMEM] + [HBM] * (4 + len(feed_weights)),
        out_specs=HBM,
        out_shape=jax.ShapeDtypeStruct(x.shape, BF16),
        scratch_shapes=[
            pltpu.VMEM(tiles, BF16),
            pltpu.VMEM((rows, width), BF16),
            pltpu.VMEM((rows, width), BF16),
            pltpu.VMEM(tiles, BF16),
            pltpu.VMEM((block * BLOCK, block * BLOCK), F32),
            pltpu.VMEM(gains.shape, BF16),
            pltpu.VMEM(w_group.shape, BF16),
            pltpu.VMEM(w_group_out.shape, BF16),
            *extra,
            pltpu.SemaphoreType.DMA((20,)),
        ],
        compiler_params=params(),
        cost_estimate=pl.CostEstimate(
            flops=2 * rows * width * width * (4 + 8 * chunk) + 8 * rows * 256 * width,
            bytes_accessed=8 << 20,
            transcendentals=rows * 256 * HEADS,
        ),
        name=f"group_attention_{chunk}",
    )(ids, x, gains, w_group, w_group_out, *feed_weights)


def feed_kernel(x_ref, gains_hbm, up_hbm, down_hbm, out_ref, x, norm, hidden, result, gains, up, down, sems):
    devices, series, patches, width = x_ref.shape
    rows = devices * patches
    rows_of = lambda s: slice(s * rows, (s + 1) * rows)
    copies = Copies(sems)
    get_gains = copies.start(gains_hbm, gains)
    get_x = [copies.start(x_ref.at[:, s], x.at[s]) for s in range(series)]
    get_up, get_down = copies.start(up_hbm, up), copies.start(down_hbm, down)
    get_gains.wait()
    gain = gains[2:3].astype(F32)
    for s in range(series):
        get_x[s].wait()
        norm[rows_of(s)] = normed(x[s].reshape(rows, width), gain)
    get_up.wait()
    get_down.wait()
    update = feed(norm, up, down, hidden)
    puts = []
    for s in range(series):
        total = x[s].reshape(rows, width).astype(F32) + update[rows_of(s)]
        result[s] = total.astype(BF16)
        puts.append(copies.start(result.at[s], out_ref.at[s, :rows]))
    for put in puts:
        put.wait()


def feed_chunk(x, gains, w_up, w_down):
    devices, series, patches, width = x.shape
    hidden = w_up.shape[1]
    part = devices * patches
    rows = series * part
    return pl.pallas_call(
        feed_kernel,
        in_specs=[HBM] * 4,
        out_specs=HBM,
        out_shape=jax.ShapeDtypeStruct((series, CHUNKS * part, width), BF16),
        scratch_shapes=[
            pltpu.VMEM((series, devices, patches, width), BF16),
            pltpu.VMEM((rows, width), BF16),
            pltpu.VMEM((rows, hidden), BF16),
            pltpu.VMEM((series, part, width), BF16),
            pltpu.VMEM(gains.shape, BF16),
            pltpu.VMEM(w_up.shape, BF16),
            pltpu.VMEM(w_down.shape, BF16),
            pltpu.SemaphoreType.DMA((20,)),
        ],
        compiler_params=params(),
        cost_estimate=pl.CostEstimate(
            flops=4 * rows * width * hidden, bytes_accessed=4 << 20, transcendentals=rows * hidden
        ),
        name="feed_forward_0",
    )(x, gains, w_up, w_down)


def place_kernel(x_ref, _, out_ref, x, get_sems, put_sems):
    series = x_ref.shape[1]
    low = out_ref.shape[1] // CHUNKS
    gets, puts = Copies(get_sems), Copies(put_sems)
    arrivals = [gets.start(x_ref.at[:, s], x.at[s]) for s in range(series)]
    leaving = []
    for s in range(series):
        arrivals[s].wait()
        rows = x.at[s].reshape(low, out_ref.shape[2])
        leaving.append(puts.start(rows, out_ref.at[s, low:]))
    for copy in leaving:
        copy.wait()


def placed(x, out):
    devices, series, patches, width = x.shape
    return pl.pallas_call(
        place_kernel,
        in_specs=[HBM] * 2,
        out_specs=HBM,
        out_shape=jax.ShapeDtypeStruct(out.shape, BF16),
        scratch_shapes=[
            pltpu.VMEM((series, devices, patches, width), BF16),
            pltpu.SemaphoreType.DMA((series,)),
            pltpu.SemaphoreType.DMA((series,)),
        ],
        input_output_aliases={1: 0},
        compiler_params=pltpu.CompilerParams(vmem_limit_bytes=4 << 20),
        name="rows_in_place",
    )(x, out)


def exchanged(blocks):
    return lax.all_to_all(blocks, "patch", split_axis=0, concat_axis=0)


def per_device(
    series_data, group_id, gains, w_time, w_time_out, w_group, w_group_out, w_up, w_down
):
    devices = lax.axis_size("patch")
    series, length, width = series_data.shape
    block = devices * series
    tables = rotary_tables(length)

    time_inputs = (devices, series_data, gains, tables, w_time, w_time_out)
    mixed_a, *kept = time_chunk(0, *time_inputs)
    there_a = exchanged(mixed_a)
    (mixed_b,) = time_chunk(1, *time_inputs, kept)
    there_b = exchanged(mixed_b)
    shape = there_a.shape
    joined = (block, shape[2], width)
    group_inputs = (group_id, gains, w_group, w_group_out)
    group_a = group_chunk(0, there_a.reshape(joined), *group_inputs)
    back_a = exchanged(group_a.reshape(shape))
    group_b = group_chunk(1, there_b.reshape(joined), *group_inputs, w_up, w_down)
    back_b = exchanged(group_b.reshape(shape))
    out = feed_chunk(back_a, gains, w_up, w_down)
    return placed(back_b, out)


def solution(mesh):
    in_specs = (P(("series", "patch"), None, None), P(), P(), P(), P(), P(), P(), P(), P())
    out_specs = P(("series", "patch"), None, None)
    return jax.shard_map(
        per_device, mesh=mesh, in_specs=in_specs, out_specs=out_specs, check_vma=False
    )
```

```python
import functools
import math

import jax
import jax.numpy as jnp
import numpy as np
from jax import lax
from jax.experimental import pallas as pl
from jax.experimental.pallas import tpu as pltpu
from jax.sharding import PartitionSpec as P

HEADS = 12
HEAD = 64
SLAB = 128
QUAD = 256
EPSILON = 1e-06
CHUNKS = 2
BLOCK = 16
BF16, F32 = jnp.bfloat16, jnp.float32
VMEM_LIMIT = 60 * 1024 * 1024

TAIL = (
    -1.0000376231361372,
    -1.1507878484871916,
    -0.4599924445285111,
    -0.05182737928832041,
    0.00708455624965549,
    -0.00047330922195818663,
)


def dot(a, b):
    return jnp.dot(a, b, preferred_element_type=F32)


def dot_t(a, b):
    return lax.dot_general(a, b, (((1,), (1,)), ((), ())), preferred_element_type=F32)


def normed(values, gain_row):
    values = values.astype(F32)
    mean_square = jnp.mean(values * values, axis=-1, keepdims=True)
    return (values * lax.rsqrt(mean_square + EPSILON) * gain_row).astype(BF16)


def gelu(x):
    size = jnp.abs(x)
    tail = jnp.full_like(size, TAIL[-1])
    for coefficient in TAIL[-2::-1]:
        tail = tail * size + coefficient
    return jnp.maximum(x, 0.0) - size * jnp.exp2(tail)


def rotary_tables(length):
    half = HEAD // 2
    frequency = 10000.0 ** (-np.arange(half) / half)
    angles = np.arange(length)[:, None] * frequency[None, :]
    cosine, sine = np.cos(angles), np.sin(angles)
    cosine = np.concatenate([cosine] * 4, axis=1).astype(np.float32)
    sine = np.concatenate([-sine, sine, -sine, sine], axis=1).astype(np.float32)
    return cosine, sine


def rotated(tensor, cosine, sine, scale=None):
    lane = lax.broadcasted_iota(jnp.int32, (tensor.shape[0], SLAB), 1)
    front = lax.rem(lane, HEAD) < HEAD // 2
    parts = []
    for start in range(0, tensor.shape[1], SLAB):
        slab = tensor[:, start : start + SLAB]
        other = jnp.where(front, pltpu.roll(slab, SLAB - 32, 1), pltpu.roll(slab, 32, 1))
        turned = slab * cosine + other * sine
        if scale is not None:
            turned = turned * scale
        parts.append(turned.astype(BF16))
    return jnp.concatenate(parts, axis=1)


QUERY_SCALE = math.log2(math.e) / math.sqrt(HEAD)
HBM = pl.BlockSpec(memory_space=pltpu.HBM)
SMEM = pl.BlockSpec(memory_space=pltpu.SMEM)


def slab_scores(queries, keys):
    first = lax.broadcasted_iota(jnp.int32, queries.shape, 1) < HEAD
    zero = jnp.zeros_like(queries)
    both = jnp.concatenate([jnp.where(first, queries, zero), jnp.where(first, zero, queries)], axis=0)
    return dot_t(both, keys)


def slab_context(scores, values):
    rows = scores.shape[0] // 2
    top = jnp.max(scores, axis=-1, keepdims=True)
    weights = jnp.exp2(scores - top).astype(BF16)
    sums = dot(weights, jnp.concatenate([values, jnp.ones_like(values)], axis=1))
    first = lax.broadcasted_iota(jnp.int32, (rows, SLAB), 1) < HEAD
    numerator = jnp.where(first, sums[:rows, :SLAB], sums[rows:, :SLAB])
    denominator = jnp.where(first, sums[:rows, SLAB:], sums[rows:, SLAB:])
    return (numerator / denominator).astype(BF16)


def pipelined(units, scores_of, context_of):
    scores = scores_of(units[0])
    for index, unit in enumerate(units):
        later = scores_of(units[index + 1]) if index + 1 < len(units) else None
        context_of(unit, scores)
        scores = later


class Copies:
    def __init__(self, sems):
        self.sems, self.used = sems, 0

    def start(self, source, target):
        copy = pltpu.make_async_copy(source, target, self.sems.at[self.used])
        self.used += 1
        copy.start()
        return copy


def time_kernel(chunk, *refs):
    if chunk == 0:
        (x_ref, gains_hbm, cos_hbm, sin_hbm, w_hbm, wo_hbm,
         mixed_ref, keys_hbm, values_hbm, later_hbm,
         x, wq, wo, cosine, sine, context, mixed, keys, values, norm, gains, wk, wv, sems) = refs
    else:
        (x_ref, cos_hbm, sin_hbm, w_hbm, wo_hbm, keys_hbm, values_hbm, later_hbm,
         mixed_ref, x, wq, wo, cosine, sine, context, mixed, keys, values, norm, sems) = refs
    series, length, width = x_ref.shape
    part = length // CHUNKS
    low = chunk * part
    quads = width // QUAD
    copies = Copies(sems)
    puts = []
    needed = []
    if chunk == 0:
        get_gains = copies.start(gains_hbm, gains)
        get_x = [copies.start(x_ref.at[s], x.at[s]) for s in range(series)]
    else:
        get_norm = copies.start(later_hbm, norm)
    for j in range(quads):
        own = slice(j * QUAD, (j + 1) * QUAD)
        group = []
        for i, target in ((1, wk), (2, wv), (0, wq)) if chunk == 0 else ((0, wq),):
            lanes = slice(i * width + j * QUAD, i * width + (j + 1) * QUAD)
            group.append(copies.start(w_hbm.at[:, lanes], target.at[:, own]))
        if j == 0:
            group.append(copies.start(cos_hbm.at[low:], cosine))
            group.append(copies.start(sin_hbm.at[low:], sine))
        if chunk > 0:
            group.append(copies.start(keys_hbm.at[:, :, own], keys.at[:, :, own]))
            group.append(copies.start(values_hbm.at[:, :, own], values.at[:, :, own]))
        needed.append(group)
    get_wo = copies.start(wo_hbm, wo)
    if chunk == 0:
        get_gains.wait()
        gain = gains[0:1].astype(F32)
        for s in range(series):
            get_x[s].wait()
            norm[s] = normed(x[s], gain)
        puts.append(copies.start(norm.at[:, part:], later_hbm))
        now = norm[:, :part].reshape(series * part, width)
        everything = norm[...].reshape(series * length, width)
        residual = lambda s: x[s, :part]
    else:
        get_x = copies.start(x_ref.at[:, low:], x)
        get_norm.wait()
        now = norm[...].reshape(series * part, width)
        residual = lambda s: x[s]
    lanes_of = lambda j: slice(j * QUAD, (j + 1) * QUAD)
    queries = {}

    def project(j):
        own = lanes_of(j)
        if chunk == 0:
            raw = dot(everything, wk[:, own])
            for s in range(series):
                keys[s, :, own] = rotated(raw[s * length : (s + 1) * length], cosine[...], sine[...])
            values[:, :, own] = dot(everything, wv[:, own]).astype(BF16).reshape(series, length, QUAD)
        raw = dot(now, wq[:, own])
        for s in range(series):
            rows = raw[s * part : (s + 1) * part]
            queries[j, s] = rotated(rows, cosine[:part], sine[:part], QUERY_SCALE)

    def scores_of(unit):
        j, start, s = unit
        own = slice(j * QUAD + start, j * QUAD + start + SLAB)
        return slab_scores(queries[j, s][:, start : start + SLAB], keys[s, :, own])

    def context_of(unit, scores):
        j, start, s = unit
        own = slice(j * QUAD + start, j * QUAD + start + SLAB)
        context[s * part : (s + 1) * part, own] = slab_context(scores, values[s, :, own])

    for copy in needed[0]:
        copy.wait()
    project(0)
    for copy in needed[1] + needed[2] + [get_wo]:
        copy.wait()
    for j in range(quads):
        if j + 1 < quads:
            project(j + 1)
        pipelined([(j, start, s) for start in range(0, QUAD, SLAB) for s in range(series)], scores_of, context_of)
        if chunk == 0 and j + 2 == quads:
            puts.append(copies.start(keys, keys_hbm))
            puts.append(copies.start(values, values_hbm))
    if chunk > 0:
        get_x.wait()
    update = dot(context[...], wo[...])
    for s in range(series):
        result = residual(s).astype(F32) + update[s * part : (s + 1) * part]
        mixed[s] = result.astype(BF16).reshape(mixed.shape[1:])
        puts.append(copies.start(mixed.at[s], mixed_ref.at[:, s]))
    for put in puts:
        put.wait()


def params(mebibytes=60):
    return pltpu.CompilerParams(vmem_limit_bytes=mebibytes * 1024 * 1024)


def time_chunk(chunk, devices, x, gains, tables, w_time, w_time_out, kept=()):
    series, length, width = x.shape
    part = length // CHUNKS
    mixed_shape = (devices, series, part // devices, width)
    rows = series * part
    table_rows = length - chunk * part
    like = jax.ShapeDtypeStruct(x.shape, BF16)
    out_shape = [jax.ShapeDtypeStruct(mixed_shape, BF16)]
    operands = [x, *tables, w_time, w_time_out, *kept]
    scratch = [
        pltpu.VMEM((series, length if chunk == 0 else part, width), BF16),
        pltpu.VMEM((width, width), BF16),
        pltpu.VMEM((width, width), BF16),
        pltpu.VMEM((table_rows, SLAB), F32),
        pltpu.VMEM((table_rows, SLAB), F32),
        pltpu.VMEM((rows, width), BF16),
        pltpu.VMEM((series, devices, part // devices, width), BF16),
        pltpu.VMEM(x.shape, BF16),
        pltpu.VMEM(x.shape, BF16),
        pltpu.VMEM((series, length if chunk == 0 else part, width), BF16),
    ]
    flops = 2 * rows * width * width * 2 + 8 * rows * length * width
    if chunk == 0:
        operands.insert(1, gains)
        out_shape += [like, like, jax.ShapeDtypeStruct((series, length - part, width), BF16)]
        scratch += [
            pltpu.VMEM(gains.shape, BF16),
            pltpu.VMEM((width, width), BF16),
            pltpu.VMEM((width, width), BF16),
        ]
        flops += 2 * series * length * width * width * 2
    return pl.pallas_call(
        functools.partial(time_kernel, chunk),
        in_specs=[HBM] * len(operands),
        out_specs=[HBM] * len(out_shape),
        out_shape=out_shape,
        scratch_shapes=scratch + [pltpu.SemaphoreType.DMA((32,))],
        compiler_params=params(),
        cost_estimate=pl.CostEstimate(
            flops=flops, bytes_accessed=8 << 20, transcendentals=rows * length * HEADS
        ),
        name=f"time_attention_{chunk}",
    )(*operands)


FF_TILE = 512


def feed(norm, up, down, hidden, first, last):
    for start in range(first, last, FF_TILE):
        own = slice(start, start + FF_TILE)
        hidden[:, own] = gelu(dot(norm[...], up[:, own])).astype(BF16)
    return dot(hidden[:, first:last], down[first:last])


def group_kernel(chunk, *refs):
    if chunk == 0:
        (ids, x_ref, gains_hbm, wg_hbm, wo_hbm, out_ref,
         x, norm, context, result, bias, gains, wg, wo, sems) = refs
    else:
        (ids, x_ref, gains_hbm, wg_hbm, wo_hbm, up_hbm, down_hbm, out_ref,
         x, norm, context, result, bias, gains, wg, wo, hidden, up, down, sems) = refs
    block, patches, width = x_ref.shape
    tiles = patches // BLOCK
    rows = block * BLOCK
    copies = Copies(sems)
    patches_of = lambda t: slice(t * BLOCK, (t + 1) * BLOCK)
    rows_of = lambda t: slice(t * rows, (t + 1) * rows)
    get_x = [copies.start(gains_hbm, gains)]
    get_x += [copies.start(x_ref.at[:, patches_of(t)], x.at[t]) for t in range(tiles)]
    quads = width // QUAD
    get_w = []
    for j in range(quads):
        parts = [slice(i * width + j * QUAD, i * width + (j + 1) * QUAD) for i in range(3)]
        get_w.append([copies.start(wg_hbm.at[:, lanes], wg.at[:, lanes]) for lanes in parts])
    get_w[-1].append(copies.start(wo_hbm, wo))
    if chunk > 0:
        get_feed = [copies.start(up_hbm, up), copies.start(down_hbm, down)]

    row = lax.broadcasted_iota(jnp.int32, (rows, rows), 0)
    column = lax.broadcasted_iota(jnp.int32, (rows, rows), 1)
    row_series, column_series = row // BLOCK, column // BLOCK
    row_group, column_group = jnp.zeros_like(row), jnp.zeros_like(row)
    first_series = lax.axis_index("series") * block
    for s in range(block):
        group = ids[first_series + s]
        row_group = jnp.where(row_series == s, group, row_group)
        column_group = jnp.where(column_series == s, group, column_group)
    same = jnp.logical_and(row_group == column_group, lax.rem(row, BLOCK) == lax.rem(column, BLOCK))
    bias[...] = jnp.where(same, 0.0, -1e30)

    get_x[0].wait()
    gain = gains[1:2].astype(F32)
    for t in range(tiles):
        get_x[1 + t].wait()
        norm[rows_of(t)] = normed(x[t].reshape(rows, width), gain)
    projected = {}

    def project(j):
        for i in range(3):
            raw = dot(norm[...], wg[:, i * width + j * QUAD : i * width + (j + 1) * QUAD])
            projected[j, i] = (raw * QUERY_SCALE if i == 0 else raw).astype(BF16)

    def scores_of(unit):
        j, start, t = unit
        lanes = slice(start, start + SLAB)
        scores = slab_scores(projected[j, 0][rows_of(t), lanes], projected[j, 1][rows_of(t), lanes])
        return scores + jnp.concatenate([bias[...], bias[...]], axis=0)

    def context_of(unit, scores):
        j, start, t = unit
        made = slab_context(scores, projected[j, 2][rows_of(t), start : start + SLAB])
        context[rows_of(t), j * QUAD + start : j * QUAD + start + SLAB] = made

    for copy in get_w[0]:
        copy.wait()
    project(0)
    for copy in get_w[1] + get_w[2]:
        copy.wait()
    for j in range(quads):
        if j + 1 < quads:
            project(j + 1)
        pipelined([(j, start, t) for start in range(0, QUAD, SLAB) for t in range(tiles)], scores_of, context_of)

    update = dot(context[...], wo[...])
    if chunk > 0:
        gain = gains[2:3].astype(F32)
        for t in range(tiles):
            total = x[t].reshape(rows, width).astype(F32) + update[rows_of(t)]
            x[t] = total.astype(BF16).reshape(block, BLOCK, width)
            norm[rows_of(t)] = normed(x[t].reshape(rows, width), gain)
        for copy in get_feed:
            copy.wait()
        update = feed(norm, up, down, hidden, 0, up.shape[1])
    puts = []
    for t in range(tiles):
        total = x[t].reshape(rows, width).astype(F32) + update[rows_of(t)]
        result[t] = total.astype(BF16).reshape(block, BLOCK, width)
        puts.append(copies.start(result.at[t], out_ref.at[:, patches_of(t)]))
    for copy in puts:
        copy.wait()


def group_chunk(chunk, x, ids, gains, w_group, w_group_out, *feed_weights):
    block, patches, width = x.shape
    rows = block * patches
    tiles = (patches // BLOCK, block, BLOCK, width)
    extra = [pltpu.VMEM(array.shape, BF16) for array in feed_weights]
    if extra:
        extra.insert(0, pltpu.VMEM((rows, feed_weights[0].shape[1]), BF16))
    return pl.pallas_call(
        functools.partial(group_kernel, chunk),
        in_specs=[SMEM] + [HBM] * (4 + len(feed_weights)),
        out_specs=HBM,
        out_shape=jax.ShapeDtypeStruct(x.shape, BF16),
        scratch_shapes=[
            pltpu.VMEM(tiles, BF16),
            pltpu.VMEM((rows, width), BF16),
            pltpu.VMEM((rows, width), BF16),
            pltpu.VMEM(tiles, BF16),
            pltpu.VMEM((block * BLOCK, block * BLOCK), F32),
            pltpu.VMEM(gains.shape, BF16),
            pltpu.VMEM(w_group.shape, BF16),
            pltpu.VMEM(w_group_out.shape, BF16),
            *extra,
            pltpu.SemaphoreType.DMA((20,)),
        ],
        compiler_params=params(),
        cost_estimate=pl.CostEstimate(
            flops=2 * rows * width * width * (4 + 8 * chunk) + 8 * rows * 256 * width,
            bytes_accessed=8 << 20,
            transcendentals=rows * 256 * HEADS,
        ),
        name=f"group_attention_{chunk}",
    )(ids, x, gains, w_group, w_group_out, *feed_weights)


def feed_kernel(x_ref, gains_hbm, up_hbm, down_hbm, out_ref, x, norm, hidden, result, gains, up, down, sems):
    devices, series, patches, width = x_ref.shape
    rows = devices * patches
    rows_of = lambda s: slice(s * rows, (s + 1) * rows)
    copies = Copies(sems)
    get_gains = copies.start(gains_hbm, gains)
    get_x = [copies.start(x_ref.at[:, s], x.at[s]) for s in range(series)]
    get_feed = [copies.start(up_hbm, up), copies.start(down_hbm, down)]
    get_gains.wait()
    gain = gains[2:3].astype(F32)
    for s in range(series):
        get_x[s].wait()
        norm[rows_of(s)] = normed(x[s].reshape(rows, width), gain)
    for copy in get_feed:
        copy.wait()
    update = feed(norm, up, down, hidden, 0, up.shape[1])
    puts = []
    for s in range(series):
        total = x[s].reshape(rows, width).astype(F32) + update[rows_of(s)]
        result[s] = total.astype(BF16)
        puts.append(copies.start(result.at[s], out_ref.at[s, :rows]))
    for put in puts:
        put.wait()


def feed_chunk(x, gains, w_up, w_down):
    devices, series, patches, width = x.shape
    hidden = w_up.shape[1]
    part = devices * patches
    rows = series * part
    return pl.pallas_call(
        feed_kernel,
        in_specs=[HBM] * 4,
        out_specs=HBM,
        out_shape=jax.ShapeDtypeStruct((series, CHUNKS * part, width), BF16),
        scratch_shapes=[
            pltpu.VMEM((series, devices, patches, width), BF16),
            pltpu.VMEM((rows, width), BF16),
            pltpu.VMEM((rows, hidden), BF16),
            pltpu.VMEM((series, part, width), BF16),
            pltpu.VMEM(gains.shape, BF16),
            pltpu.VMEM(w_up.shape, BF16),
            pltpu.VMEM(w_down.shape, BF16),
            pltpu.SemaphoreType.DMA((20,)),
        ],
        compiler_params=params(),
        cost_estimate=pl.CostEstimate(
            flops=4 * rows * width * hidden, bytes_accessed=4 << 20, transcendentals=rows * hidden
        ),
        name="feed_forward_0",
    )(x, gains, w_up, w_down)


def place_kernel(x_ref, _, out_ref, x, get_sems, put_sems):
    series = x_ref.shape[1]
    low = out_ref.shape[1] // CHUNKS
    gets, puts = Copies(get_sems), Copies(put_sems)
    arrivals = [gets.start(x_ref.at[:, s], x.at[s]) for s in range(series)]
    leaving = []
    for s in range(series):
        arrivals[s].wait()
        rows = x.at[s].reshape(low, out_ref.shape[2])
        leaving.append(puts.start(rows, out_ref.at[s, low:]))
    for copy in leaving:
        copy.wait()


def placed(x, out):
    devices, series, patches, width = x.shape
    return pl.pallas_call(
        place_kernel,
        in_specs=[HBM] * 2,
        out_specs=HBM,
        out_shape=jax.ShapeDtypeStruct(out.shape, BF16),
        scratch_shapes=[
            pltpu.VMEM((series, devices, patches, width), BF16),
            pltpu.SemaphoreType.DMA((series,)),
            pltpu.SemaphoreType.DMA((series,)),
        ],
        input_output_aliases={1: 0},
        compiler_params=pltpu.CompilerParams(vmem_limit_bytes=4 << 20),
        name="rows_in_place",
    )(x, out)


def exchanged(blocks):
    return lax.all_to_all(blocks, "patch", split_axis=0, concat_axis=0)


def per_device(
    series_data, group_id, gains, w_time, w_time_out, w_group, w_group_out, w_up, w_down
):
    devices = lax.axis_size("patch")
    series, length, width = series_data.shape
    block = devices * series
    tables = rotary_tables(length)

    time_inputs = (devices, series_data, gains, tables, w_time, w_time_out)
    mixed_a, *kept = time_chunk(0, *time_inputs)
    there_a = exchanged(mixed_a)
    (mixed_b,) = time_chunk(1, *time_inputs, kept)
    there_b = exchanged(mixed_b)
    shape = there_a.shape
    joined = (block, shape[2], width)
    group_inputs = (group_id, gains, w_group, w_group_out)
    group_a = group_chunk(0, there_a.reshape(joined), *group_inputs)
    back_a = exchanged(group_a.reshape(shape))
    group_b = group_chunk(1, there_b.reshape(joined), *group_inputs, w_up, w_down)
    back_b = exchanged(group_b.reshape(shape))
    out = feed_chunk(back_a, gains, w_up, w_down)
    return placed(back_b, out)


def solution(mesh):
    in_specs = (P(("series", "patch"), None, None), P(), P(), P(), P(), P(), P(), P(), P())
    out_specs = P(("series", "patch"), None, None)
    return jax.shard_map(
        per_device, mesh=mesh, in_specs=in_specs, out_specs=out_specs, check_vma=False
    )
```

```python
import functools
import math

import jax
import jax.numpy as jnp
import numpy as np
from jax import lax
from jax.experimental import pallas as pl
from jax.experimental.pallas import tpu as pltpu
from jax.sharding import PartitionSpec as P

HEADS = 12
HEAD = 64
SLAB = 128
QUAD = 256
EPSILON = 1e-06
CHUNKS = 2
BLOCK = 16
BF16, F32 = jnp.bfloat16, jnp.float32
VMEM_LIMIT = 60 * 1024 * 1024

TAIL = (
    -1.0000376231361372,
    -1.1507878484871916,
    -0.4599924445285111,
    -0.05182737928832041,
    0.00708455624965549,
    -0.00047330922195818663,
)


def dot(a, b):
    return jnp.dot(a, b, preferred_element_type=F32)


def dot_t(a, b):
    return lax.dot_general(a, b, (((1,), (1,)), ((), ())), preferred_element_type=F32)


def normed(values, gain_row):
    values = values.astype(F32)
    mean_square = jnp.mean(values * values, axis=-1, keepdims=True)
    return (values * lax.rsqrt(mean_square + EPSILON) * gain_row).astype(BF16)


def gelu(x):
    size = jnp.abs(x)
    tail = jnp.full_like(size, TAIL[-1])
    for coefficient in TAIL[-2::-1]:
        tail = tail * size + coefficient
    return jnp.maximum(x, 0.0) - size * jnp.exp2(tail)


def rotary_tables(length):
    half = HEAD // 2
    frequency = 10000.0 ** (-np.arange(half) / half)
    angles = np.arange(length)[:, None] * frequency[None, :]
    cosine, sine = np.cos(angles), np.sin(angles)
    cosine = np.concatenate([cosine] * 4, axis=1).astype(np.float32)
    sine = np.concatenate([-sine, sine, -sine, sine], axis=1).astype(np.float32)
    return cosine, sine


def rotated(tensor, cosine, sine, scale=None):
    lane = lax.broadcasted_iota(jnp.int32, (tensor.shape[0], SLAB), 1)
    front = lax.rem(lane, HEAD) < HEAD // 2
    parts = []
    for start in range(0, tensor.shape[1], SLAB):
        slab = tensor[:, start : start + SLAB]
        other = jnp.where(front, pltpu.roll(slab, SLAB - 32, 1), pltpu.roll(slab, 32, 1))
        turned = slab * cosine + other * sine
        if scale is not None:
            turned = turned * scale
        parts.append(turned.astype(BF16))
    return jnp.concatenate(parts, axis=1)


QUERY_SCALE = math.log2(math.e) / math.sqrt(HEAD)
HBM = pl.BlockSpec(memory_space=pltpu.HBM)
SMEM = pl.BlockSpec(memory_space=pltpu.SMEM)


def slab_scores(queries, keys):
    first = lax.broadcasted_iota(jnp.int32, queries.shape, 1) < HEAD
    zero = jnp.zeros_like(queries)
    both = jnp.concatenate([jnp.where(first, queries, zero), jnp.where(first, zero, queries)], axis=0)
    return dot_t(both, keys)


def slab_context(scores, values):
    rows = scores.shape[0] // 2
    top = jnp.max(scores, axis=-1, keepdims=True)
    weights = jnp.exp2(scores - top).astype(BF16)
    sums = dot(weights, jnp.concatenate([values, jnp.ones_like(values)], axis=1))
    first = lax.broadcasted_iota(jnp.int32, (rows, SLAB), 1) < HEAD
    numerator = jnp.where(first, sums[:rows, :SLAB], sums[rows:, :SLAB])
    denominator = jnp.where(first, sums[:rows, SLAB:], sums[rows:, SLAB:])
    return (numerator / denominator).astype(BF16)


def pipelined(units, scores_of, context_of):
    scores = scores_of(units[0])
    for index, unit in enumerate(units):
        later = scores_of(units[index + 1]) if index + 1 < len(units) else None
        context_of(unit, scores)
        scores = later


def group_bias(ids, block):
    rows = block * BLOCK
    row = lax.broadcasted_iota(jnp.int32, (rows, rows), 0)
    column = lax.broadcasted_iota(jnp.int32, (rows, rows), 1)
    row_series, column_series = row // BLOCK, column // BLOCK
    row_group, column_group = jnp.zeros_like(row), jnp.zeros_like(row)
    first_series = lax.axis_index("series") * block
    for s in range(block):
        group = ids[first_series + s]
        row_group = jnp.where(row_series == s, group, row_group)
        column_group = jnp.where(column_series == s, group, column_group)
    same = jnp.logical_and(row_group == column_group, lax.rem(row, BLOCK) == lax.rem(column, BLOCK))
    return jnp.where(same, 0.0, -1e30)


class Copies:
    def __init__(self, sems):
        self.sems, self.used = sems, 0

    def start(self, source, target):
        copy = pltpu.make_async_copy(source, target, self.sems.at[self.used])
        self.used += 1
        copy.start()
        return copy


def time_kernel(chunk, *refs):
    if chunk == 0:
        (x_ref, gains_hbm, cos_hbm, sin_hbm, w_hbm, wo_hbm,
         mixed_ref, keys_hbm, values_hbm, later_hbm,
         x, wq, wo, cosine, sine, context, mixed, keys, values, norm, gains, wk, wv, sems) = refs
    else:
        (ids, x_ref, cos_hbm, sin_hbm, w_hbm, wo_hbm, keys_hbm, values_hbm, later_hbm,
         mixed_ref, bias_hbm, x, wq, wo, cosine, sine, context, mixed, keys, values, norm, bias, sems) = refs
    series, length, width = x_ref.shape
    part = length // CHUNKS
    low = chunk * part
    quads = width // QUAD
    copies = Copies(sems)
    puts = []
    needed = []
    if chunk == 0:
        get_gains = copies.start(gains_hbm, gains)
        get_x = [copies.start(x_ref.at[s], x.at[s]) for s in range(series)]
    else:
        get_norm = copies.start(later_hbm, norm)
    for j in range(quads):
        own = slice(j * QUAD, (j + 1) * QUAD)
        group = []
        for i, target in ((1, wk), (2, wv), (0, wq)) if chunk == 0 else ((0, wq),):
            lanes = slice(i * width + j * QUAD, i * width + (j + 1) * QUAD)
            group.append(copies.start(w_hbm.at[:, lanes], target.at[:, own]))
        if j == 0:
            group.append(copies.start(cos_hbm.at[low:], cosine))
            group.append(copies.start(sin_hbm.at[low:], sine))
        if chunk > 0:
            group.append(copies.start(keys_hbm.at[:, :, own], keys.at[:, :, own]))
            group.append(copies.start(values_hbm.at[:, :, own], values.at[:, :, own]))
        needed.append(group)
    get_wo = copies.start(wo_hbm, wo)
    if chunk == 0:
        get_gains.wait()
        gain = gains[0:1].astype(F32)
        for s in range(series):
            get_x[s].wait()
            norm[s] = normed(x[s], gain)
        puts.append(copies.start(norm.at[:, part:], later_hbm))
        now = norm[:, :part].reshape(series * part, width)
        everything = norm[...].reshape(series * length, width)
        residual = lambda s: x[s, :part]
    else:
        get_x = copies.start(x_ref.at[:, low:], x)
        bias[...] = group_bias(ids, mixed_ref.shape[0] * series)
        puts.append(copies.start(bias, bias_hbm))
        get_norm.wait()
        now = norm[...].reshape(series * part, width)
        residual = lambda s: x[s]
    lanes_of = lambda j: slice(j * QUAD, (j + 1) * QUAD)
    queries = {}

    def project(j):
        own = lanes_of(j)
        if chunk == 0:
            raw = dot(everything, wk[:, own])
            for s in range(series):
                keys[s, :, own] = rotated(raw[s * length : (s + 1) * length], cosine[...], sine[...])
            values[:, :, own] = dot(everything, wv[:, own]).astype(BF16).reshape(series, length, QUAD)
        raw = dot(now, wq[:, own])
        for s in range(series):
            rows = raw[s * part : (s + 1) * part]
            queries[j, s] = rotated(rows, cosine[:part], sine[:part], QUERY_SCALE)

    def scores_of(unit):
        j, start, s = unit
        own = slice(j * QUAD + start, j * QUAD + start + SLAB)
        return slab_scores(queries[j, s][:, start : start + SLAB], keys[s, :, own])

    def context_of(unit, scores):
        j, start, s = unit
        own = slice(j * QUAD + start, j * QUAD + start + SLAB)
        context[s * part : (s + 1) * part, own] = slab_context(scores, values[s, :, own])

    for copy in needed[0]:
        copy.wait()
    project(0)
    for copy in needed[1] + needed[2] + [get_wo]:
        copy.wait()
    for j in range(quads):
        if j + 1 < quads:
            project(j + 1)
        pipelined([(j, start, s) for start in range(0, QUAD, SLAB) for s in range(series)], scores_of, context_of)
        if chunk == 0 and j + 2 == quads:
            puts.append(copies.start(keys, keys_hbm))
            puts.append(copies.start(values, values_hbm))
    if chunk > 0:
        get_x.wait()
    update = dot(context[...], wo[...])
    for s in range(series):
        result = residual(s).astype(F32) + update[s * part : (s + 1) * part]
        mixed[s] = result.astype(BF16).reshape(mixed.shape[1:])
        puts.append(copies.start(mixed.at[s], mixed_ref.at[:, s]))
    for put in puts:
        put.wait()


def params(mebibytes=60):
    return pltpu.CompilerParams(vmem_limit_bytes=mebibytes * 1024 * 1024)


def time_chunk(chunk, devices, x, gains, tables, w_time, w_time_out, ids=None, kept=()):
    series, length, width = x.shape
    part = length // CHUNKS
    mixed_shape = (devices, series, part // devices, width)
    rows = series * part
    table_rows = length - chunk * part
    like = jax.ShapeDtypeStruct(x.shape, BF16)
    out_shape = [jax.ShapeDtypeStruct(mixed_shape, BF16)]
    operands = [x, *tables, w_time, w_time_out, *kept]
    scratch = [
        pltpu.VMEM((series, length if chunk == 0 else part, width), BF16),
        pltpu.VMEM((width, width), BF16),
        pltpu.VMEM((width, width), BF16),
        pltpu.VMEM((table_rows, SLAB), F32),
        pltpu.VMEM((table_rows, SLAB), F32),
        pltpu.VMEM((rows, width), BF16),
        pltpu.VMEM((series, devices, part // devices, width), BF16),
        pltpu.VMEM(x.shape, BF16),
        pltpu.VMEM(x.shape, BF16),
        pltpu.VMEM((series, length if chunk == 0 else part, width), BF16),
    ]
    flops = 2 * rows * width * width * 2 + 8 * rows * length * width
    if chunk == 0:
        in_specs = [HBM] * 6
        operands.insert(1, gains)
        out_shape += [like, like, jax.ShapeDtypeStruct((series, length - part, width), BF16)]
        scratch += [
            pltpu.VMEM(gains.shape, BF16),
            pltpu.VMEM((width, width), BF16),
            pltpu.VMEM((width, width), BF16),
        ]
        flops += 2 * series * length * width * width * 2
    else:
        pairs = (devices * series * BLOCK,) * 2
        in_specs = [SMEM] + [HBM] * len(operands)
        operands.insert(0, ids)
        out_shape.append(jax.ShapeDtypeStruct(pairs, F32))
        scratch.append(pltpu.VMEM(pairs, F32))
    return pl.pallas_call(
        functools.partial(time_kernel, chunk),
        in_specs=in_specs,
        out_specs=[HBM] * len(out_shape),
        out_shape=out_shape,
        scratch_shapes=scratch + [pltpu.SemaphoreType.DMA((32,))],
        compiler_params=params(),
        cost_estimate=pl.CostEstimate(
            flops=flops, bytes_accessed=8 << 20, transcendentals=rows * length * HEADS
        ),
        name=f"time_attention_{chunk}",
    )(*operands)


FF_TILE = 256


def feed(norm, up, down, hidden, first, last):
    for start in range(first, last, FF_TILE):
        own = slice(start, start + FF_TILE)
        hidden[:, own] = gelu(dot(norm[...], up[:, own])).astype(BF16)
    return dot(hidden[:, first:last], down[first:last])


def group_kernel(chunk, *refs):
    if chunk == 0:
        (bias_hbm, x_ref, gains_hbm, wg_hbm, wo_hbm, out_ref,
         x, norm, context, result, bias, gains, wg, wo, sems) = refs
    else:
        (bias_hbm, x_ref, gains_hbm, wg_hbm, wo_hbm, up_hbm, down_hbm, out_ref,
         x, norm, context, result, bias, gains, wg, wo, hidden, up, down, sems) = refs
    block, patches, width = x_ref.shape
    tiles = patches // BLOCK
    rows = block * BLOCK
    copies = Copies(sems)
    patches_of = lambda t: slice(t * BLOCK, (t + 1) * BLOCK)
    rows_of = lambda t: slice(t * rows, (t + 1) * rows)
    get_x = [copies.start(gains_hbm, gains)]
    get_x += [copies.start(x_ref.at[:, patches_of(t)], x.at[t]) for t in range(tiles)]
    quads = width // QUAD
    get_w = []
    for j in range(quads):
        parts = [slice(i * width + j * QUAD, i * width + (j + 1) * QUAD) for i in range(3)]
        get_w.append([copies.start(wg_hbm.at[:, lanes], wg.at[:, lanes]) for lanes in parts])
        if j == 0:
            get_w[0].append(copies.start(bias_hbm, bias))
    get_w[-1].append(copies.start(wo_hbm, wo))
    if chunk > 0:
        get_feed = [copies.start(up_hbm, up), copies.start(down_hbm, down)]

    get_x[0].wait()
    gain = gains[1:2].astype(F32)
    for t in range(tiles):
        get_x[1 + t].wait()
        norm[rows_of(t)] = normed(x[t].reshape(rows, width), gain)
    projected = {}

    def project(j):
        for i in range(3):
            raw = dot(norm[...], wg[:, i * width + j * QUAD : i * width + (j + 1) * QUAD])
            projected[j, i] = (raw * QUERY_SCALE if i == 0 else raw).astype(BF16)

    def scores_of(unit):
        j, start, t = unit
        lanes = slice(start, start + SLAB)
        scores = slab_scores(projected[j, 0][rows_of(t), lanes], projected[j, 1][rows_of(t), lanes])
        return scores + jnp.concatenate([bias[...], bias[...]], axis=0)

    def context_of(unit, scores):
        j, start, t = unit
        made = slab_context(scores, projected[j, 2][rows_of(t), start : start + SLAB])
        context[rows_of(t), j * QUAD + start : j * QUAD + start + SLAB] = made

    for copy in get_w[0]:
        copy.wait()
    project(0)
    for copy in get_w[1] + get_w[2]:
        copy.wait()
    for j in range(quads):
        if j + 1 < quads:
            project(j + 1)
        pipelined([(j, start, t) for start in range(0, QUAD, SLAB) for t in range(tiles)], scores_of, context_of)

    if chunk > 0:
        for copy in get_feed:
            copy.wait()
    update = dot(context[...], wo[...])
    if chunk > 0:
        gain = gains[2:3].astype(F32)
        for t in range(tiles):
            total = x[t].reshape(rows, width).astype(F32) + update[rows_of(t)]
            x[t] = total.astype(BF16).reshape(block, BLOCK, width)
            norm[rows_of(t)] = normed(x[t].reshape(rows, width), gain)
        update = feed(norm, up, down, hidden, 0, up.shape[1])
    puts = []
    for t in range(tiles):
        total = x[t].reshape(rows, width).astype(F32) + update[rows_of(t)]
        result[t] = total.astype(BF16).reshape(block, BLOCK, width)
        puts.append(copies.start(result.at[t], out_ref.at[:, patches_of(t)]))
    for copy in puts:
        copy.wait()


def group_chunk(chunk, x, bias, gains, w_group, w_group_out, *feed_weights):
    block, patches, width = x.shape
    rows = block * patches
    tiles = (patches // BLOCK, block, BLOCK, width)
    extra = [pltpu.VMEM(array.shape, BF16) for array in feed_weights]
    if extra:
        extra.insert(0, pltpu.VMEM((rows, feed_weights[0].shape[1]), BF16))
    return pl.pallas_call(
        functools.partial(group_kernel, chunk),
        in_specs=[HBM] * (5 + len(feed_weights)),
        out_specs=HBM,
        out_shape=jax.ShapeDtypeStruct(x.shape, BF16),
        scratch_shapes=[
            pltpu.VMEM(tiles, BF16),
            pltpu.VMEM((rows, width), BF16),
            pltpu.VMEM((rows, width), BF16),
            pltpu.VMEM(tiles, BF16),
            pltpu.VMEM(bias.shape, F32),
            pltpu.VMEM(gains.shape, BF16),
            pltpu.VMEM(w_group.shape, BF16),
            pltpu.VMEM(w_group_out.shape, BF16),
            *extra,
            pltpu.SemaphoreType.DMA((20,)),
        ],
        compiler_params=params(),
        cost_estimate=pl.CostEstimate(
            flops=2 * rows * width * width * (4 + 8 * chunk) + 8 * rows * 256 * width,
            bytes_accessed=8 << 20,
            transcendentals=rows * 256 * HEADS,
        ),
        name=f"group_attention_{chunk}",
    )(bias, x, gains, w_group, w_group_out, *feed_weights)


def feed_kernel(x_ref, gains_hbm, up_hbm, down_hbm, out_ref, x, norm, hidden, result, gains, up, down, sems):
    devices, series, patches, width = x_ref.shape
    rows = devices * patches
    rows_of = lambda s: slice(s * rows, (s + 1) * rows)
    copies = Copies(sems)
    get_gains = copies.start(gains_hbm, gains)
    get_x = [copies.start(x_ref.at[:, s], x.at[s]) for s in range(series)]
    get_feed = [copies.start(up_hbm, up), copies.start(down_hbm, down)]
    get_gains.wait()
    gain = gains[2:3].astype(F32)
    for s in range(series):
        get_x[s].wait()
        norm[rows_of(s)] = normed(x[s].reshape(rows, width), gain)
    for copy in get_feed:
        copy.wait()
    update = feed(norm, up, down, hidden, 0, up.shape[1])
    puts = []
    for s in range(series):
        total = x[s].reshape(rows, width).astype(F32) + update[rows_of(s)]
        result[s] = total.astype(BF16)
        puts.append(copies.start(result.at[s], out_ref.at[s, :rows]))
    for put in puts:
        put.wait()


def feed_chunk(x, gains, w_up, w_down):
    devices, series, patches, width = x.shape
    hidden = w_up.shape[1]
    part = devices * patches
    rows = series * part
    return pl.pallas_call(
        feed_kernel,
        in_specs=[HBM] * 4,
        out_specs=HBM,
        out_shape=jax.ShapeDtypeStruct((series, CHUNKS * part, width), BF16),
        scratch_shapes=[
            pltpu.VMEM((series, devices, patches, width), BF16),
            pltpu.VMEM((rows, width), BF16),
            pltpu.VMEM((rows, hidden), BF16),
            pltpu.VMEM((series, part, width), BF16),
            pltpu.VMEM(gains.shape, BF16),
            pltpu.VMEM(w_up.shape, BF16),
            pltpu.VMEM(w_down.shape, BF16),
            pltpu.SemaphoreType.DMA((20,)),
        ],
        compiler_params=params(),
        cost_estimate=pl.CostEstimate(
            flops=4 * rows * width * hidden, bytes_accessed=4 << 20, transcendentals=rows * hidden
        ),
        name="feed_forward_0",
    )(x, gains, w_up, w_down)


def place_kernel(x_ref, _, out_ref, x, get_sems, put_sems):
    series = x_ref.shape[1]
    low = out_ref.shape[1] // CHUNKS
    gets, puts = Copies(get_sems), Copies(put_sems)
    arrivals = [gets.start(x_ref.at[:, s], x.at[s]) for s in range(series)]
    leaving = []
    for s in range(series):
        arrivals[s].wait()
        rows = x.at[s].reshape(low, out_ref.shape[2])
        leaving.append(puts.start(rows, out_ref.at[s, low:]))
    for copy in leaving:
        copy.wait()


def placed(x, out):
    devices, series, patches, width = x.shape
    return pl.pallas_call(
        place_kernel,
        in_specs=[HBM] * 2,
        out_specs=HBM,
        out_shape=jax.ShapeDtypeStruct(out.shape, BF16),
        scratch_shapes=[
            pltpu.VMEM((series, devices, patches, width), BF16),
            pltpu.SemaphoreType.DMA((series,)),
            pltpu.SemaphoreType.DMA((series,)),
        ],
        input_output_aliases={1: 0},
        compiler_params=pltpu.CompilerParams(vmem_limit_bytes=4 << 20),
        name="rows_in_place",
    )(x, out)


def exchanged(blocks):
    return lax.all_to_all(blocks, "patch", split_axis=0, concat_axis=0)


def per_device(
    series_data, group_id, gains, w_time, w_time_out, w_group, w_group_out, w_up, w_down
):
    devices = lax.axis_size("patch")
    series, length, width = series_data.shape
    block = devices * series
    tables = rotary_tables(length)

    time_inputs = (devices, series_data, gains, tables, w_time, w_time_out)
    mixed_a, *kept = time_chunk(0, *time_inputs)
    there_a = exchanged(mixed_a)
    mixed_b, bias = time_chunk(1, *time_inputs, group_id, kept)
    there_b = exchanged(mixed_b)
    shape = there_a.shape
    joined = (block, shape[2], width)
    group_inputs = (bias, gains, w_group, w_group_out)
    group_a = group_chunk(0, there_a.reshape(joined), *group_inputs)
    back_a = exchanged(group_a.reshape(shape))
    group_b = group_chunk(1, there_b.reshape(joined), *group_inputs, w_up, w_down)
    back_b = exchanged(group_b.reshape(shape))
    out = feed_chunk(back_a, gains, w_up, w_down)
    return placed(back_b, out)


def solution(mesh):
    in_specs = (P(("series", "patch"), None, None), P(), P(), P(), P(), P(), P(), P(), P())
    out_specs = P(("series", "patch"), None, None)
    return jax.shard_map(
        per_device, mesh=mesh, in_specs=in_specs, out_specs=out_specs, check_vma=False
    )
```

```python
import functools
import math

import jax
import jax.numpy as jnp
import numpy as np
from jax import lax
from jax.experimental import pallas as pl
from jax.experimental.pallas import tpu as pltpu
from jax.sharding import PartitionSpec as P

HEADS = 12
HEAD = 64
SLAB = 128
QUAD = 256
EPSILON = 1e-06
CHUNKS = 2
BLOCK = 16
BF16, F32 = jnp.bfloat16, jnp.float32
VMEM_LIMIT = 60 * 1024 * 1024

TAIL = (
    -1.0000376231361372,
    -1.1507878484871916,
    -0.4599924445285111,
    -0.05182737928832041,
    0.00708455624965549,
    -0.00047330922195818663,
)


def dot(a, b):
    return jnp.dot(a, b, preferred_element_type=F32)


def dot_t(a, b):
    return lax.dot_general(a, b, (((1,), (1,)), ((), ())), preferred_element_type=F32)


def normed(values, gain_row):
    values = values.astype(F32)
    mean_square = jnp.mean(values * values, axis=-1, keepdims=True)
    return (values * lax.rsqrt(mean_square + EPSILON) * gain_row).astype(BF16)


def gelu(x):
    size = jnp.abs(x)
    tail = jnp.full_like(size, TAIL[-1])
    for coefficient in TAIL[-2::-1]:
        tail = tail * size + coefficient
    return jnp.maximum(x, 0.0) - size * jnp.exp2(tail)


def rotary_tables(length):
    half = HEAD // 2
    frequency = 10000.0 ** (-np.arange(half) / half)
    angles = np.arange(length)[:, None] * frequency[None, :]
    cosine, sine = np.cos(angles), np.sin(angles)
    cosine = np.concatenate([cosine] * 4, axis=1).astype(np.float32)
    sine = np.concatenate([-sine, sine, -sine, sine], axis=1).astype(np.float32)
    return cosine, sine


def rotated(tensor, cosine, sine, scale=None):
    lane = lax.broadcasted_iota(jnp.int32, (tensor.shape[0], SLAB), 1)
    front = lax.rem(lane, HEAD) < HEAD // 2
    parts = []
    for start in range(0, tensor.shape[1], SLAB):
        slab = tensor[:, start : start + SLAB]
        other = jnp.where(front, pltpu.roll(slab, SLAB - 32, 1), pltpu.roll(slab, 32, 1))
        turned = slab * cosine + other * sine
        if scale is not None:
            turned = turned * scale
        parts.append(turned.astype(BF16))
    return jnp.concatenate(parts, axis=1)


QUERY_SCALE = math.log2(math.e) / math.sqrt(HEAD)
HBM = pl.BlockSpec(memory_space=pltpu.HBM)
SMEM = pl.BlockSpec(memory_space=pltpu.SMEM)


def slab_scores(queries, keys):
    first = lax.broadcasted_iota(jnp.int32, queries.shape, 1) < HEAD
    zero = jnp.zeros_like(queries)
    both = jnp.concatenate([jnp.where(first, queries, zero), jnp.where(first, zero, queries)], axis=0)
    return dot_t(both, keys)


def slab_context(scores, values):
    rows = scores.shape[0] // 2
    top = jnp.max(scores, axis=-1, keepdims=True)
    weights = jnp.exp2(scores - top).astype(BF16)
    sums = dot(weights, jnp.concatenate([values, jnp.ones_like(values)], axis=1))
    first = lax.broadcasted_iota(jnp.int32, (rows, SLAB), 1) < HEAD
    numerator = jnp.where(first, sums[:rows, :SLAB], sums[rows:, :SLAB])
    denominator = jnp.where(first, sums[:rows, SLAB:], sums[rows:, SLAB:])
    return (numerator / denominator).astype(BF16)


def pipelined(units, scores_of, context_of):
    scores = scores_of(units[0])
    for index, unit in enumerate(units):
        later = scores_of(units[index + 1]) if index + 1 < len(units) else None
        context_of(unit, scores)
        scores = later


def group_bias(ids, block):
    rows = block * BLOCK
    row = lax.broadcasted_iota(jnp.int32, (rows, rows), 0)
    column = lax.broadcasted_iota(jnp.int32, (rows, rows), 1)
    row_series, column_series = row // BLOCK, column // BLOCK
    row_group, column_group = jnp.zeros_like(row), jnp.zeros_like(row)
    first_series = lax.axis_index("series") * block
    for s in range(block):
        group = ids[first_series + s]
        row_group = jnp.where(row_series == s, group, row_group)
        column_group = jnp.where(column_series == s, group, column_group)
    same = jnp.logical_and(row_group == column_group, lax.rem(row, BLOCK) == lax.rem(column, BLOCK))
    return jnp.where(same, 0.0, -1e30)


class Copies:
    def __init__(self, sems):
        self.sems, self.used = sems, 0

    def start(self, source, target):
        copy = pltpu.make_async_copy(source, target, self.sems.at[self.used])
        self.used += 1
        copy.start()
        return copy


def time_kernel(chunk, *refs):
    if chunk == 0:
        (x_ref, gains_hbm, cos_hbm, sin_hbm, w_hbm, wo_hbm,
         mixed_ref, keys_hbm, values_hbm, later_hbm,
         x, wq, wo, cosine, sine, context, mixed, keys, values, norm, gains, wk, wv, sems) = refs
    else:
        (ids, x_ref, cos_hbm, sin_hbm, w_hbm, wo_hbm, keys_hbm, values_hbm, later_hbm,
         mixed_ref, bias_hbm, x, wq, wo, cosine, sine, context, mixed, keys, values, norm, bias, sems) = refs
    series, length, width = x_ref.shape
    part = length // CHUNKS
    low = chunk * part
    quads = width // QUAD
    copies = Copies(sems)
    puts = []
    needed = []
    if chunk == 0:
        get_gains = copies.start(gains_hbm, gains)
        get_x = [copies.start(x_ref.at[s], x.at[s]) for s in range(series)]
    else:
        get_norm = copies.start(later_hbm, norm)
    for j in range(quads):
        own = slice(j * QUAD, (j + 1) * QUAD)
        group = []
        for i, target in ((1, wk), (2, wv), (0, wq)) if chunk == 0 else ((0, wq),):
            lanes = slice(i * width + j * QUAD, i * width + (j + 1) * QUAD)
            group.append(copies.start(w_hbm.at[:, lanes], target.at[:, own]))
        if j == 0:
            group.append(copies.start(cos_hbm.at[low:], cosine))
            group.append(copies.start(sin_hbm.at[low:], sine))
        if chunk > 0:
            group.append(copies.start(keys_hbm.at[:, :, own], keys.at[:, :, own]))
            group.append(copies.start(values_hbm.at[:, :, own], values.at[:, :, own]))
        needed.append(group)
    get_wo = copies.start(wo_hbm, wo)
    if chunk == 0:
        get_gains.wait()
        gain = gains[0:1].astype(F32)
        for s in range(series):
            get_x[s].wait()
            norm[s] = normed(x[s], gain)
        puts.append(copies.start(norm.at[:, part:], later_hbm))
        now = norm[:, :part].reshape(series * part, width)
        everything = norm[...].reshape(series * length, width)
        residual = lambda s: x[s, :part]
    else:
        get_x = copies.start(x_ref.at[:, low:], x)
        bias[...] = group_bias(ids, mixed_ref.shape[0] * series)
        puts.append(copies.start(bias, bias_hbm))
        get_norm.wait()
        now = norm[...].reshape(series * part, width)
        residual = lambda s: x[s]
    for copy in needed[0] + needed[1] + needed[2] + [get_wo]:
        copy.wait()

    @pl.loop(0, quads)
    def _(j):
        own = pl.ds(pl.multiple_of(j * QUAD, QUAD), QUAD)
        if chunk == 0:
            raw = dot(everything, wk[:, own])
            own_values = dot(everything, wv[:, own]).astype(BF16).reshape(series, length, QUAD)
            own_keys = [
                rotated(raw[s * length : (s + 1) * length], cosine[...], sine[...]) for s in range(series)
            ]
            values[:, :, own] = own_values
            for s in range(series):
                keys[s, :, own] = own_keys[s]
        else:
            own_values = values[:, :, own]
            own_keys = [keys[s, :, own] for s in range(series)]
        raw = dot(now, wq[:, own])
        queries = [
            rotated(raw[s * part : (s + 1) * part], cosine[:part], sine[:part], QUERY_SCALE)
            for s in range(series)
        ]

        def scores_of(unit):
            start, s = unit
            lanes = slice(start, start + SLAB)
            return slab_scores(queries[s][:, lanes], own_keys[s][:, lanes])

        def context_of(unit, scores):
            start, s = unit
            made = slab_context(scores, own_values[s][:, start : start + SLAB])
            target = pl.ds(pl.multiple_of(j * QUAD + start, SLAB), SLAB)
            context[s * part : (s + 1) * part, target] = made

        pipelined([(start, s) for start in range(0, QUAD, SLAB) for s in range(series)], scores_of, context_of)

    if chunk == 0:
        puts.append(copies.start(keys, keys_hbm))
        puts.append(copies.start(values, values_hbm))
    if chunk > 0:
        get_x.wait()
    update = dot(context[...], wo[...])
    for s in range(series):
        result = residual(s).astype(F32) + update[s * part : (s + 1) * part]
        mixed[s] = result.astype(BF16).reshape(mixed.shape[1:])
        puts.append(copies.start(mixed.at[s], mixed_ref.at[:, s]))
    for put in puts:
        put.wait()


def params(mebibytes=60):
    return pltpu.CompilerParams(vmem_limit_bytes=mebibytes * 1024 * 1024)


def time_chunk(chunk, devices, x, gains, tables, w_time, w_time_out, ids=None, kept=()):
    series, length, width = x.shape
    part = length // CHUNKS
    mixed_shape = (devices, series, part // devices, width)
    rows = series * part
    table_rows = length - chunk * part
    like = jax.ShapeDtypeStruct(x.shape, BF16)
    out_shape = [jax.ShapeDtypeStruct(mixed_shape, BF16)]
    operands = [x, *tables, w_time, w_time_out, *kept]
    scratch = [
        pltpu.VMEM((series, length if chunk == 0 else part, width), BF16),
        pltpu.VMEM((width, width), BF16),
        pltpu.VMEM((width, width), BF16),
        pltpu.VMEM((table_rows, SLAB), F32),
        pltpu.VMEM((table_rows, SLAB), F32),
        pltpu.VMEM((rows, width), BF16),
        pltpu.VMEM((series, devices, part // devices, width), BF16),
        pltpu.VMEM(x.shape, BF16),
        pltpu.VMEM(x.shape, BF16),
        pltpu.VMEM((series, length if chunk == 0 else part, width), BF16),
    ]
    flops = 2 * rows * width * width * 2 + 8 * rows * length * width
    if chunk == 0:
        in_specs = [HBM] * 6
        operands.insert(1, gains)
        out_shape += [like, like, jax.ShapeDtypeStruct((series, length - part, width), BF16)]
        scratch += [
            pltpu.VMEM(gains.shape, BF16),
            pltpu.VMEM((width, width), BF16),
            pltpu.VMEM((width, width), BF16),
        ]
        flops += 2 * series * length * width * width * 2
    else:
        pairs = (devices * series * BLOCK,) * 2
        in_specs = [SMEM] + [HBM] * len(operands)
        operands.insert(0, ids)
        out_shape.append(jax.ShapeDtypeStruct(pairs, F32))
        scratch.append(pltpu.VMEM(pairs, F32))
    return pl.pallas_call(
        functools.partial(time_kernel, chunk),
        in_specs=in_specs,
        out_specs=[HBM] * len(out_shape),
        out_shape=out_shape,
        scratch_shapes=scratch + [pltpu.SemaphoreType.DMA((32,))],
        compiler_params=params(),
        cost_estimate=pl.CostEstimate(
            flops=flops, bytes_accessed=8 << 20, transcendentals=rows * length * HEADS
        ),
        name=f"time_attention_{chunk}",
    )(*operands)


FF_TILE = 256


FF_BODY = 1024


def feed(norm, up, down, total):
    @pl.loop(0, up.shape[1] // FF_BODY)
    def _(j):
        hidden = []
        for start in range(0, FF_BODY, FF_TILE):
            own = pl.ds(pl.multiple_of(j * FF_BODY + start, FF_TILE), FF_TILE)
            hidden.append(gelu(dot(norm[...], up[:, own])).astype(BF16))
        own = pl.ds(pl.multiple_of(j * FF_BODY, FF_BODY), FF_BODY)
        total[...] += dot(jnp.concatenate(hidden, axis=1), down[own, :])


def group_kernel(chunk, *refs):
    if chunk == 0:
        (bias_hbm, x_ref, gains_hbm, wg_hbm, wo_hbm, out_ref,
         x, norm, context, result, bias, gains, wg, wo, sems) = refs
    else:
        (bias_hbm, x_ref, gains_hbm, wg_hbm, wo_hbm, up_hbm, down_hbm, out_ref,
         x, norm, context, result, bias, gains, wg, wo, hidden, up, down, sems) = refs
    block, patches, width = x_ref.shape
    tiles = patches // BLOCK
    rows = block * BLOCK
    copies = Copies(sems)
    patches_of = lambda t: slice(t * BLOCK, (t + 1) * BLOCK)
    rows_of = lambda t: slice(t * rows, (t + 1) * rows)
    get_x = [copies.start(gains_hbm, gains)]
    get_x += [copies.start(x_ref.at[:, patches_of(t)], x.at[t]) for t in range(tiles)]
    quads = width // QUAD
    get_w = []
    for j in range(quads):
        parts = [slice(i * width + j * QUAD, i * width + (j + 1) * QUAD) for i in range(3)]
        get_w.append([copies.start(wg_hbm.at[:, lanes], wg.at[:, lanes]) for lanes in parts])
        if j == 0:
            get_w[0].append(copies.start(bias_hbm, bias))
    get_w[-1].append(copies.start(wo_hbm, wo))
    if chunk > 0:
        get_feed = [copies.start(up_hbm, up), copies.start(down_hbm, down)]

    get_x[0].wait()
    gain = gains[1:2].astype(F32)
    for t in range(tiles):
        get_x[1 + t].wait()
        norm[rows_of(t)] = normed(x[t].reshape(rows, width), gain)
    for copies_of_quad in get_w:
        for copy in copies_of_quad:
            copy.wait()

    @pl.loop(0, quads)
    def _(j):
        def project(i):
            return dot(norm[...], wg[:, pl.ds(pl.multiple_of(i * width + j * QUAD, QUAD), QUAD)])

        queries = (project(0) * QUERY_SCALE).astype(BF16)
        own_keys = project(1).astype(BF16)
        own_values = project(2).astype(BF16)

        def scores_of(unit):
            start, t = unit
            lanes = slice(start, start + SLAB)
            scores = slab_scores(queries[rows_of(t), lanes], own_keys[rows_of(t), lanes])
            return scores + jnp.concatenate([bias[...], bias[...]], axis=0)

        def context_of(unit, scores):
            start, t = unit
            made = slab_context(scores, own_values[rows_of(t), start : start + SLAB])
            context[rows_of(t), pl.ds(pl.multiple_of(j * QUAD + start, SLAB), SLAB)] = made

        pipelined([(start, t) for start in range(0, QUAD, SLAB) for t in range(tiles)], scores_of, context_of)

    if chunk > 0:
        for copy in get_feed:
            copy.wait()
    update = dot(context[...], wo[...])
    if chunk > 0:
        gain = gains[2:3].astype(F32)
        for t in range(tiles):
            total = x[t].reshape(rows, width).astype(F32) + update[rows_of(t)]
            x[t] = total.astype(BF16).reshape(block, BLOCK, width)
            norm[rows_of(t)] = normed(x[t].reshape(rows, width), gain)
            hidden[rows_of(t)] = x[t].reshape(rows, width).astype(F32)
        feed(norm, up, down, hidden)
    puts = []
    for t in range(tiles):
        if chunk > 0:
            total = hidden[rows_of(t)]
        else:
            total = x[t].reshape(rows, width).astype(F32) + update[rows_of(t)]
        result[t] = total.astype(BF16).reshape(block, BLOCK, width)
        puts.append(copies.start(result.at[t], out_ref.at[:, patches_of(t)]))
    for copy in puts:
        copy.wait()


def group_chunk(chunk, x, bias, gains, w_group, w_group_out, *feed_weights):
    block, patches, width = x.shape
    rows = block * patches
    tiles = (patches // BLOCK, block, BLOCK, width)
    extra = [pltpu.VMEM(array.shape, BF16) for array in feed_weights]
    if extra:
        extra.insert(0, pltpu.VMEM((rows, width), F32))
    return pl.pallas_call(
        functools.partial(group_kernel, chunk),
        in_specs=[HBM] * (5 + len(feed_weights)),
        out_specs=HBM,
        out_shape=jax.ShapeDtypeStruct(x.shape, BF16),
        scratch_shapes=[
            pltpu.VMEM(tiles, BF16),
            pltpu.VMEM((rows, width), BF16),
            pltpu.VMEM((rows, width), BF16),
            pltpu.VMEM(tiles, BF16),
            pltpu.VMEM(bias.shape, F32),
            pltpu.VMEM(gains.shape, BF16),
            pltpu.VMEM(w_group.shape, BF16),
            pltpu.VMEM(w_group_out.shape, BF16),
            *extra,
            pltpu.SemaphoreType.DMA((20,)),
        ],
        compiler_params=params(),
        cost_estimate=pl.CostEstimate(
            flops=2 * rows * width * width * (4 + 8 * chunk) + 8 * rows * 256 * width,
            bytes_accessed=8 << 20,
            transcendentals=rows * 256 * HEADS,
        ),
        name=f"group_attention_{chunk}",
    )(bias, x, gains, w_group, w_group_out, *feed_weights)


def feed_kernel(x_ref, gains_hbm, up_hbm, down_hbm, out_ref, x, norm, hidden, result, gains, up, down, sems):
    devices, series, patches, width = x_ref.shape
    rows = devices * patches
    rows_of = lambda s: slice(s * rows, (s + 1) * rows)
    copies = Copies(sems)
    get_gains = copies.start(gains_hbm, gains)
    get_x = [copies.start(x_ref.at[:, s], x.at[s]) for s in range(series)]
    get_feed = [copies.start(up_hbm, up), copies.start(down_hbm, down)]
    get_gains.wait()
    gain = gains[2:3].astype(F32)
    for s in range(series):
        get_x[s].wait()
        norm[rows_of(s)] = normed(x[s].reshape(rows, width), gain)
        hidden[rows_of(s)] = x[s].reshape(rows, width).astype(F32)
    for copy in get_feed:
        copy.wait()
    feed(norm, up, down, hidden)
    puts = []
    for s in range(series):
        result[s] = hidden[rows_of(s)].astype(BF16)
        puts.append(copies.start(result.at[s], out_ref.at[s, :rows]))
    for put in puts:
        put.wait()


def feed_chunk(x, gains, w_up, w_down):
    devices, series, patches, width = x.shape
    hidden = w_up.shape[1]
    part = devices * patches
    rows = series * part
    return pl.pallas_call(
        feed_kernel,
        in_specs=[HBM] * 4,
        out_specs=HBM,
        out_shape=jax.ShapeDtypeStruct((series, CHUNKS * part, width), BF16),
        scratch_shapes=[
            pltpu.VMEM((series, devices, patches, width), BF16),
            pltpu.VMEM((rows, width), BF16),
            pltpu.VMEM((rows, width), F32),
            pltpu.VMEM((series, part, width), BF16),
            pltpu.VMEM(gains.shape, BF16),
            pltpu.VMEM(w_up.shape, BF16),
            pltpu.VMEM(w_down.shape, BF16),
            pltpu.SemaphoreType.DMA((20,)),
        ],
        compiler_params=params(),
        cost_estimate=pl.CostEstimate(
            flops=4 * rows * width * hidden, bytes_accessed=4 << 20, transcendentals=rows * hidden
        ),
        name="feed_forward_0",
    )(x, gains, w_up, w_down)


def place_kernel(x_ref, _, out_ref, x, get_sems, put_sems):
    series = x_ref.shape[1]
    low = out_ref.shape[1] // CHUNKS
    gets, puts = Copies(get_sems), Copies(put_sems)
    arrivals = [gets.start(x_ref.at[:, s], x.at[s]) for s in range(series)]
    leaving = []
    for s in range(series):
        arrivals[s].wait()
        rows = x.at[s].reshape(low, out_ref.shape[2])
        leaving.append(puts.start(rows, out_ref.at[s, low:]))
    for copy in leaving:
        copy.wait()


def placed(x, out):
    devices, series, patches, width = x.shape
    return pl.pallas_call(
        place_kernel,
        in_specs=[HBM] * 2,
        out_specs=HBM,
        out_shape=jax.ShapeDtypeStruct(out.shape, BF16),
        scratch_shapes=[
            pltpu.VMEM((series, devices, patches, width), BF16),
            pltpu.SemaphoreType.DMA((series,)),
            pltpu.SemaphoreType.DMA((series,)),
        ],
        input_output_aliases={1: 0},
        compiler_params=pltpu.CompilerParams(vmem_limit_bytes=4 << 20),
        name="rows_in_place",
    )(x, out)


def exchanged(blocks):
    return lax.all_to_all(blocks, "patch", split_axis=0, concat_axis=0)


def per_device(
    series_data, group_id, gains, w_time, w_time_out, w_group, w_group_out, w_up, w_down
):
    devices = lax.axis_size("patch")
    series, length, width = series_data.shape
    block = devices * series
    tables = rotary_tables(length)

    time_inputs = (devices, series_data, gains, tables, w_time, w_time_out)
    mixed_a, *kept = time_chunk(0, *time_inputs)
    there_a = exchanged(mixed_a)
    mixed_b, bias = time_chunk(1, *time_inputs, group_id, kept)
    there_b = exchanged(mixed_b)
    shape = there_a.shape
    joined = (block, shape[2], width)
    group_inputs = (bias, gains, w_group, w_group_out)
    group_a = group_chunk(0, there_a.reshape(joined), *group_inputs)
    back_a = exchanged(group_a.reshape(shape))
    group_b = group_chunk(1, there_b.reshape(joined), *group_inputs, w_up, w_down)
    back_b = exchanged(group_b.reshape(shape))
    out = feed_chunk(back_a, gains, w_up, w_down)
    return placed(back_b, out)


def solution(mesh):
    in_specs = (P(("series", "patch"), None, None), P(), P(), P(), P(), P(), P(), P(), P())
    out_specs = P(("series", "patch"), None, None)
    return jax.shard_map(
        per_device, mesh=mesh, in_specs=in_specs, out_specs=out_specs, check_vma=False
    )
```

```python
import functools
import math

import jax
import jax.numpy as jnp
import numpy as np
from jax import lax
from jax.experimental import pallas as pl
from jax.experimental.pallas import tpu as pltpu
from jax.sharding import PartitionSpec as P

HEADS = 12
HEAD = 64
SLAB = 128
QUAD = 256
EPSILON = 1e-06
CHUNKS = 2
BLOCK = 16
BF16, F32 = jnp.bfloat16, jnp.float32
VMEM_LIMIT = 60 * 1024 * 1024

TAIL = (
    -1.0000376231361372,
    -1.1507878484871916,
    -0.4599924445285111,
    -0.05182737928832041,
    0.00708455624965549,
    -0.00047330922195818663,
)


def dot(a, b):
    return jnp.dot(a, b, preferred_element_type=F32)


def dot_t(a, b):
    return lax.dot_general(a, b, (((1,), (1,)), ((), ())), preferred_element_type=F32)


def normed(values, gain_row):
    values = values.astype(F32)
    mean_square = jnp.mean(values * values, axis=-1, keepdims=True)
    return (values * lax.rsqrt(mean_square + EPSILON) * gain_row).astype(BF16)


def gelu(x):
    size = jnp.abs(x)
    tail = jnp.full_like(size, TAIL[-1])
    for coefficient in TAIL[-2::-1]:
        tail = tail * size + coefficient
    return jnp.maximum(x, 0.0) - size * jnp.exp2(tail)


def rotary_tables(length):
    half = HEAD // 2
    frequency = 10000.0 ** (-np.arange(half) / half)
    angles = np.arange(length)[:, None] * frequency[None, :]
    cosine, sine = np.cos(angles), np.sin(angles)
    cosine = np.concatenate([cosine] * 4, axis=1).astype(np.float32)
    sine = np.concatenate([-sine, sine, -sine, sine], axis=1).astype(np.float32)
    return cosine, sine


def rotated(tensor, cosine, sine, scale=None):
    lane = lax.broadcasted_iota(jnp.int32, (tensor.shape[0], SLAB), 1)
    front = lax.rem(lane, HEAD) < HEAD // 2
    parts = []
    for start in range(0, tensor.shape[1], SLAB):
        slab = tensor[:, start : start + SLAB]
        other = jnp.where(front, pltpu.roll(slab, SLAB - 32, 1), pltpu.roll(slab, 32, 1))
        turned = slab * cosine + other * sine
        if scale is not None:
            turned = turned * scale
        parts.append(turned.astype(BF16))
    return jnp.concatenate(parts, axis=1)


QUERY_SCALE = math.log2(math.e) / math.sqrt(HEAD)
HBM = pl.BlockSpec(memory_space=pltpu.HBM)
SMEM = pl.BlockSpec(memory_space=pltpu.SMEM)


def slab_scores(queries, keys):
    first = lax.broadcasted_iota(jnp.int32, queries.shape, 1) < HEAD
    zero = jnp.zeros_like(queries)
    both = jnp.concatenate([jnp.where(first, queries, zero), jnp.where(first, zero, queries)], axis=0)
    return dot_t(both, keys)


def slab_context(scores, values):
    rows = scores.shape[0] // 2
    top = jnp.max(scores, axis=-1, keepdims=True)
    weights = jnp.exp2(scores - top).astype(BF16)
    sums = dot(weights, jnp.concatenate([values, jnp.ones_like(values)], axis=1))
    first = lax.broadcasted_iota(jnp.int32, (rows, SLAB), 1) < HEAD
    numerator = jnp.where(first, sums[:rows, :SLAB], sums[rows:, :SLAB])
    denominator = jnp.where(first, sums[:rows, SLAB:], sums[rows:, SLAB:])
    return (numerator / denominator).astype(BF16)


def pipelined(units, scores_of, context_of):
    scores = scores_of(units[0])
    for index, unit in enumerate(units):
        later = scores_of(units[index + 1]) if index + 1 < len(units) else None
        context_of(unit, scores)
        scores = later


def group_bias(ids, block):
    rows = block * BLOCK
    row = lax.broadcasted_iota(jnp.int32, (rows, rows), 0)
    column = lax.broadcasted_iota(jnp.int32, (rows, rows), 1)
    row_series, column_series = row // BLOCK, column // BLOCK
    row_group, column_group = jnp.zeros_like(row), jnp.zeros_like(row)
    first_series = lax.axis_index("series") * block
    for s in range(block):
        group = ids[first_series + s]
        row_group = jnp.where(row_series == s, group, row_group)
        column_group = jnp.where(column_series == s, group, column_group)
    same = jnp.logical_and(row_group == column_group, lax.rem(row, BLOCK) == lax.rem(column, BLOCK))
    return jnp.where(same, 0.0, -1e30)


class Copies:
    def __init__(self, sems):
        self.sems, self.used = sems, 0

    def start(self, source, target):
        copy = pltpu.make_async_copy(source, target, self.sems.at[self.used])
        self.used += 1
        copy.start()
        return copy


def time_kernel(chunk, *refs):
    if chunk == 0:
        (x_ref, gains_hbm, cos_hbm, sin_hbm, w_hbm, wo_hbm,
         mixed_ref, keys_hbm, values_hbm, later_hbm,
         x, wq, wo, cosine, sine, context, mixed, keys, values, norm, gains, wk, wv, sems) = refs
    else:
        (ids, x_ref, cos_hbm, sin_hbm, w_hbm, wo_hbm, keys_hbm, values_hbm, later_hbm,
         mixed_ref, bias_hbm, x, wq, wo, cosine, sine, context, mixed, keys, values, norm, bias, sems) = refs
    series, length, width = x_ref.shape
    part = length // CHUNKS
    low = chunk * part
    quads = width // QUAD
    copies = Copies(sems)
    puts = []
    needed = []
    if chunk == 0:
        get_gains = copies.start(gains_hbm, gains)
        get_x = [copies.start(x_ref.at[s], x.at[s]) for s in range(series)]
    else:
        get_norm = copies.start(later_hbm, norm)
    for j in range(quads):
        own = slice(j * QUAD, (j + 1) * QUAD)
        group = []
        for i, target in ((1, wk), (2, wv), (0, wq)) if chunk == 0 else ((0, wq),):
            lanes = slice(i * width + j * QUAD, i * width + (j + 1) * QUAD)
            group.append(copies.start(w_hbm.at[:, lanes], target.at[:, own]))
        if j == 0:
            group.append(copies.start(cos_hbm.at[low:], cosine))
            group.append(copies.start(sin_hbm.at[low:], sine))
        if chunk > 0:
            group.append(copies.start(keys_hbm.at[:, :, own], keys.at[:, :, own]))
            group.append(copies.start(values_hbm.at[:, :, own], values.at[:, :, own]))
        needed.append(group)
    get_wo = copies.start(wo_hbm, wo)
    if chunk == 0:
        get_gains.wait()
        gain = gains[0:1].astype(F32)
        for s in range(series):
            get_x[s].wait()
            norm[s] = normed(x[s], gain)
        puts.append(copies.start(norm.at[:, part:], later_hbm))
        now = norm[:, :part].reshape(series * part, width)
        everything = norm[...].reshape(series * length, width)
        residual = lambda s: x[s, :part]
    else:
        get_x = copies.start(x_ref.at[:, low:], x)
        bias[...] = group_bias(ids, mixed_ref.shape[0] * series)
        puts.append(copies.start(bias, bias_hbm))
        get_norm.wait()
        now = norm[...].reshape(series * part, width)
        residual = lambda s: x[s]
    if chunk == 0:
        lanes_of = lambda j: slice(j * QUAD, (j + 1) * QUAD)
        queries = {}

        def project(j):
            own = lanes_of(j)
            raw = dot(everything, wk[:, own])
            for s in range(series):
                keys[s, :, own] = rotated(raw[s * length : (s + 1) * length], cosine[...], sine[...])
            values[:, :, own] = dot(everything, wv[:, own]).astype(BF16).reshape(series, length, QUAD)
            raw = dot(now, wq[:, own])
            for s in range(series):
                rows = raw[s * part : (s + 1) * part]
                queries[j, s] = rotated(rows, cosine[:part], sine[:part], QUERY_SCALE)

        def scores_of(unit):
            j, start, s = unit
            own = slice(j * QUAD + start, j * QUAD + start + SLAB)
            return slab_scores(queries[j, s][:, start : start + SLAB], keys[s, :, own])

        def context_of(unit, scores):
            j, start, s = unit
            own = slice(j * QUAD + start, j * QUAD + start + SLAB)
            context[s * part : (s + 1) * part, own] = slab_context(scores, values[s, :, own])

        for copy in needed[0]:
            copy.wait()
        project(0)
        for copy in needed[1] + needed[2] + [get_wo]:
            copy.wait()
        for j in range(quads):
            if j + 1 < quads:
                project(j + 1)
            pipelined([(j, start, s) for start in range(0, QUAD, SLAB) for s in range(series)], scores_of, context_of)
            if j + 2 == quads:
                puts.append(copies.start(keys, keys_hbm))
                puts.append(copies.start(values, values_hbm))
    else:
        for copy in needed[0] + needed[1] + needed[2] + [get_wo]:
            copy.wait()

        @pl.loop(0, quads)
        def _(j):
            own = pl.ds(pl.multiple_of(j * QUAD, QUAD), QUAD)
            own_values = values[:, :, own]
            own_keys = [keys[s, :, own] for s in range(series)]
            raw = dot(now, wq[:, own])
            queries = [
                rotated(raw[s * part : (s + 1) * part], cosine[:part], sine[:part], QUERY_SCALE)
                for s in range(series)
            ]

            def scores_of(unit):
                start, s = unit
                lanes = slice(start, start + SLAB)
                return slab_scores(queries[s][:, lanes], own_keys[s][:, lanes])

            def context_of(unit, scores):
                start, s = unit
                made = slab_context(scores, own_values[s][:, start : start + SLAB])
                target = pl.ds(pl.multiple_of(j * QUAD + start, SLAB), SLAB)
                context[s * part : (s + 1) * part, target] = made

            pipelined([(start, s) for start in range(0, QUAD, SLAB) for s in range(series)], scores_of, context_of)

    if chunk > 0:
        get_x.wait()
    update = dot(context[...], wo[...])
    for s in range(series):
        result = residual(s).astype(F32) + update[s * part : (s + 1) * part]
        mixed[s] = result.astype(BF16).reshape(mixed.shape[1:])
        puts.append(copies.start(mixed.at[s], mixed_ref.at[:, s]))
    for put in puts:
        put.wait()


def params(mebibytes=60):
    return pltpu.CompilerParams(vmem_limit_bytes=mebibytes * 1024 * 1024)


def time_chunk(chunk, devices, x, gains, tables, w_time, w_time_out, ids=None, kept=()):
    series, length, width = x.shape
    part = length // CHUNKS
    mixed_shape = (devices, series, part // devices, width)
    rows = series * part
    table_rows = length - chunk * part
    like = jax.ShapeDtypeStruct(x.shape, BF16)
    out_shape = [jax.ShapeDtypeStruct(mixed_shape, BF16)]
    operands = [x, *tables, w_time, w_time_out, *kept]
    scratch = [
        pltpu.VMEM((series, length if chunk == 0 else part, width), BF16),
        pltpu.VMEM((width, width), BF16),
        pltpu.VMEM((width, width), BF16),
        pltpu.VMEM((table_rows, SLAB), F32),
        pltpu.VMEM((table_rows, SLAB), F32),
        pltpu.VMEM((rows, width), BF16),
        pltpu.VMEM((series, devices, part // devices, width), BF16),
        pltpu.VMEM(x.shape, BF16),
        pltpu.VMEM(x.shape, BF16),
        pltpu.VMEM((series, length if chunk == 0 else part, width), BF16),
    ]
    flops = 2 * rows * width * width * 2 + 8 * rows * length * width
    if chunk == 0:
        in_specs = [HBM] * 6
        operands.insert(1, gains)
        out_shape += [like, like, jax.ShapeDtypeStruct((series, length - part, width), BF16)]
        scratch += [
            pltpu.VMEM(gains.shape, BF16),
            pltpu.VMEM((width, width), BF16),
            pltpu.VMEM((width, width), BF16),
        ]
        flops += 2 * series * length * width * width * 2
    else:
        pairs = (devices * series * BLOCK,) * 2
        in_specs = [SMEM] + [HBM] * len(operands)
        operands.insert(0, ids)
        out_shape.append(jax.ShapeDtypeStruct(pairs, F32))
        scratch.append(pltpu.VMEM(pairs, F32))
    return pl.pallas_call(
        functools.partial(time_kernel, chunk),
        in_specs=in_specs,
        out_specs=[HBM] * len(out_shape),
        out_shape=out_shape,
        scratch_shapes=scratch + [pltpu.SemaphoreType.DMA((32,))],
        compiler_params=params(),
        cost_estimate=pl.CostEstimate(
            flops=flops, bytes_accessed=8 << 20, transcendentals=rows * length * HEADS
        ),
        name=f"time_attention_{chunk}",
    )(*operands)


FF_TILE = 256


FF_BODY = 1024


def feed(norm, up, down, total):
    @pl.loop(0, up.shape[1] // FF_BODY)
    def _(j):
        hidden = []
        for start in range(0, FF_BODY, FF_TILE):
            own = pl.ds(pl.multiple_of(j * FF_BODY + start, FF_TILE), FF_TILE)
            hidden.append(gelu(dot(norm[...], up[:, own])).astype(BF16))
        own = pl.ds(pl.multiple_of(j * FF_BODY, FF_BODY), FF_BODY)
        total[...] += dot(jnp.concatenate(hidden, axis=1), down[own, :])


def group_kernel(chunk, *refs):
    if chunk == 0:
        (bias_hbm, x_ref, gains_hbm, wg_hbm, wo_hbm, out_ref,
         x, norm, context, result, bias, gains, wg, wo, sems) = refs
    else:
        (bias_hbm, x_ref, gains_hbm, wg_hbm, wo_hbm, up_hbm, down_hbm, out_ref,
         x, norm, context, result, bias, gains, wg, wo, hidden, up, down, sems) = refs
    block, patches, width = x_ref.shape
    tiles = patches // BLOCK
    rows = block * BLOCK
    copies = Copies(sems)
    patches_of = lambda t: slice(t * BLOCK, (t + 1) * BLOCK)
    rows_of = lambda t: slice(t * rows, (t + 1) * rows)
    get_x = [copies.start(gains_hbm, gains)]
    get_x += [copies.start(x_ref.at[:, patches_of(t)], x.at[t]) for t in range(tiles)]
    quads = width // QUAD
    get_w = []
    for j in range(quads):
        parts = [slice(i * width + j * QUAD, i * width + (j + 1) * QUAD) for i in range(3)]
        get_w.append([copies.start(wg_hbm.at[:, lanes], wg.at[:, lanes]) for lanes in parts])
        if j == 0:
            get_w[0].append(copies.start(bias_hbm, bias))
    get_w[-1].append(copies.start(wo_hbm, wo))
    if chunk > 0:
        get_feed = [copies.start(up_hbm, up), copies.start(down_hbm, down)]

    get_x[0].wait()
    gain = gains[1:2].astype(F32)
    for t in range(tiles):
        get_x[1 + t].wait()
        norm[rows_of(t)] = normed(x[t].reshape(rows, width), gain)
    for copies_of_quad in get_w:
        for copy in copies_of_quad:
            copy.wait()

    @pl.loop(0, quads)
    def _(j):
        def project(i):
            return dot(norm[...], wg[:, pl.ds(pl.multiple_of(i * width + j * QUAD, QUAD), QUAD)])

        queries = (project(0) * QUERY_SCALE).astype(BF16)
        own_keys = project(1).astype(BF16)
        own_values = project(2).astype(BF16)

        def scores_of(unit):
            start, t = unit
            lanes = slice(start, start + SLAB)
            scores = slab_scores(queries[rows_of(t), lanes], own_keys[rows_of(t), lanes])
            return scores + jnp.concatenate([bias[...], bias[...]], axis=0)

        def context_of(unit, scores):
            start, t = unit
            made = slab_context(scores, own_values[rows_of(t), start : start + SLAB])
            context[rows_of(t), pl.ds(pl.multiple_of(j * QUAD + start, SLAB), SLAB)] = made

        pipelined([(start, t) for start in range(0, QUAD, SLAB) for t in range(tiles)], scores_of, context_of)

    if chunk > 0:
        for copy in get_feed:
            copy.wait()
    update = dot(context[...], wo[...])
    if chunk > 0:
        gain = gains[2:3].astype(F32)
        for t in range(tiles):
            total = x[t].reshape(rows, width).astype(F32) + update[rows_of(t)]
            x[t] = total.astype(BF16).reshape(block, BLOCK, width)
            norm[rows_of(t)] = normed(x[t].reshape(rows, width), gain)
            hidden[rows_of(t)] = x[t].reshape(rows, width).astype(F32)
        feed(norm, up, down, hidden)
    puts = []
    for t in range(tiles):
        if chunk > 0:
            total = hidden[rows_of(t)]
        else:
            total = x[t].reshape(rows, width).astype(F32) + update[rows_of(t)]
        result[t] = total.astype(BF16).reshape(block, BLOCK, width)
        puts.append(copies.start(result.at[t], out_ref.at[:, patches_of(t)]))
    for copy in puts:
        copy.wait()


def group_chunk(chunk, x, bias, gains, w_group, w_group_out, *feed_weights):
    block, patches, width = x.shape
    rows = block * patches
    tiles = (patches // BLOCK, block, BLOCK, width)
    extra = [pltpu.VMEM(array.shape, BF16) for array in feed_weights]
    if extra:
        extra.insert(0, pltpu.VMEM((rows, width), F32))
    return pl.pallas_call(
        functools.partial(group_kernel, chunk),
        in_specs=[HBM] * (5 + len(feed_weights)),
        out_specs=HBM,
        out_shape=jax.ShapeDtypeStruct(x.shape, BF16),
        scratch_shapes=[
            pltpu.VMEM(tiles, BF16),
            pltpu.VMEM((rows, width), BF16),
            pltpu.VMEM((rows, width), BF16),
            pltpu.VMEM(tiles, BF16),
            pltpu.VMEM(bias.shape, F32),
            pltpu.VMEM(gains.shape, BF16),
            pltpu.VMEM(w_group.shape, BF16),
            pltpu.VMEM(w_group_out.shape, BF16),
            *extra,
            pltpu.SemaphoreType.DMA((20,)),
        ],
        compiler_params=params(),
        cost_estimate=pl.CostEstimate(
            flops=2 * rows * width * width * (4 + 8 * chunk) + 8 * rows * 256 * width,
            bytes_accessed=8 << 20,
            transcendentals=rows * 256 * HEADS,
        ),
        name=f"group_attention_{chunk}",
    )(bias, x, gains, w_group, w_group_out, *feed_weights)


def feed_kernel(x_ref, gains_hbm, up_hbm, down_hbm, out_ref, x, norm, hidden, result, gains, up, down, sems):
    devices, series, patches, width = x_ref.shape
    rows = devices * patches
    rows_of = lambda s: slice(s * rows, (s + 1) * rows)
    copies = Copies(sems)
    get_gains = copies.start(gains_hbm, gains)
    get_x = [copies.start(x_ref.at[:, s], x.at[s]) for s in range(series)]
    get_feed = [copies.start(up_hbm, up), copies.start(down_hbm, down)]
    get_gains.wait()
    gain = gains[2:3].astype(F32)
    for s in range(series):
        get_x[s].wait()
        norm[rows_of(s)] = normed(x[s].reshape(rows, width), gain)
        hidden[rows_of(s)] = x[s].reshape(rows, width).astype(F32)
    for copy in get_feed:
        copy.wait()
    feed(norm, up, down, hidden)
    puts = []
    for s in range(series):
        result[s] = hidden[rows_of(s)].astype(BF16)
        puts.append(copies.start(result.at[s], out_ref.at[s, :rows]))
    for put in puts:
        put.wait()


def feed_chunk(x, gains, w_up, w_down):
    devices, series, patches, width = x.shape
    hidden = w_up.shape[1]
    part = devices * patches
    rows = series * part
    return pl.pallas_call(
        feed_kernel,
        in_specs=[HBM] * 4,
        out_specs=HBM,
        out_shape=jax.ShapeDtypeStruct((series, CHUNKS * part, width), BF16),
        scratch_shapes=[
            pltpu.VMEM((series, devices, patches, width), BF16),
            pltpu.VMEM((rows, width), BF16),
            pltpu.VMEM((rows, width), F32),
            pltpu.VMEM((series, part, width), BF16),
            pltpu.VMEM(gains.shape, BF16),
            pltpu.VMEM(w_up.shape, BF16),
            pltpu.VMEM(w_down.shape, BF16),
            pltpu.SemaphoreType.DMA((20,)),
        ],
        compiler_params=params(),
        cost_estimate=pl.CostEstimate(
            flops=4 * rows * width * hidden, bytes_accessed=4 << 20, transcendentals=rows * hidden
        ),
        name="feed_forward_0",
    )(x, gains, w_up, w_down)


def place_kernel(x_ref, _, out_ref, x, get_sems, put_sems):
    series = x_ref.shape[1]
    low = out_ref.shape[1] // CHUNKS
    gets, puts = Copies(get_sems), Copies(put_sems)
    arrivals = [gets.start(x_ref.at[:, s], x.at[s]) for s in range(series)]
    leaving = []
    for s in range(series):
        arrivals[s].wait()
        rows = x.at[s].reshape(low, out_ref.shape[2])
        leaving.append(puts.start(rows, out_ref.at[s, low:]))
    for copy in leaving:
        copy.wait()


def placed(x, out):
    devices, series, patches, width = x.shape
    return pl.pallas_call(
        place_kernel,
        in_specs=[HBM] * 2,
        out_specs=HBM,
        out_shape=jax.ShapeDtypeStruct(out.shape, BF16),
        scratch_shapes=[
            pltpu.VMEM((series, devices, patches, width), BF16),
            pltpu.SemaphoreType.DMA((series,)),
            pltpu.SemaphoreType.DMA((series,)),
        ],
        input_output_aliases={1: 0},
        compiler_params=pltpu.CompilerParams(vmem_limit_bytes=4 << 20),
        name="rows_in_place",
    )(x, out)


def exchanged(blocks):
    return lax.all_to_all(blocks, "patch", split_axis=0, concat_axis=0)


def per_device(
    series_data, group_id, gains, w_time, w_time_out, w_group, w_group_out, w_up, w_down
):
    devices = lax.axis_size("patch")
    series, length, width = series_data.shape
    block = devices * series
    tables = rotary_tables(length)

    time_inputs = (devices, series_data, gains, tables, w_time, w_time_out)
    mixed_a, *kept = time_chunk(0, *time_inputs)
    there_a = exchanged(mixed_a)
    mixed_b, bias = time_chunk(1, *time_inputs, group_id, kept)
    there_b = exchanged(mixed_b)
    shape = there_a.shape
    joined = (block, shape[2], width)
    group_inputs = (bias, gains, w_group, w_group_out)
    group_a = group_chunk(0, there_a.reshape(joined), *group_inputs)
    back_a = exchanged(group_a.reshape(shape))
    group_b = group_chunk(1, there_b.reshape(joined), *group_inputs, w_up, w_down)
    back_b = exchanged(group_b.reshape(shape))
    out = feed_chunk(back_a, gains, w_up, w_down)
    return placed(back_b, out)


def solution(mesh):
    in_specs = (P(("series", "patch"), None, None), P(), P(), P(), P(), P(), P(), P(), P())
    out_specs = P(("series", "patch"), None, None)
    return jax.shard_map(
        per_device, mesh=mesh, in_specs=in_specs, out_specs=out_specs, check_vma=False
    )
```
